32 devices in a mesh: seq: 8 (over z, x), kv: 4 (over y, core).
Axes of the slice: x: 2, y: 2, z: 4, core: 2. Of those that a mesh axis runs over, the one named last changes fastest.
Arguments:
- tokens: bfloat16 [1, 4096, 2048], P(None, 'seq'), may hold values from -6 to 6
- attention_norm_gain: bfloat16 [2048], P('seq'), may hold values from 0.5 to 1.5
- query_weight: bfloat16 [2048, 2048], P('seq', 'kv'), may hold values from -0.125 to 0.125
- key_value_weight: bfloat16 [2, 2048, 512], P(None, 'seq', 'kv'), may hold values from -0.125 to 0.125
- output_weight: bfloat16 [2048, 2048], P(('kv', 'seq')), may hold values from -0.5 to 0.5
- adapter_down_matrices: bfloat16 [3, 2048, 8], P(None, 'seq'), may hold values from -0.125 to 0.125
- adapter_query_up: bfloat16 [8, 2048], P(None, ('kv', 'seq')), may hold values from -2 to 2
- adapter_key_value_up: bfloat16 [2, 8, 512], P(None, None, ('kv', 'seq')), may hold values from -2 to 2
- adapter_output_down: bfloat16 [2048, 8], P(('kv', 'seq')), may hold values from -0.5 to 0.5
- adapter_output_up: bfloat16 [8, 2048], P(None, 'seq'), may hold values from -2 to 2
- query_feature_matrix: bfloat16 [32, 64, 64], P('kv', 'seq'), may hold values from -1 to 1
- key_feature_matrix: bfloat16 [8, 64, 64], P('kv', 'seq'), may hold values from -1 to 1
- feedforward_norm_gain: bfloat16 [2048], P('seq'), may hold values from 0.5 to 1.5
- gate_weight: bfloat16 [2048, 8192], P('seq', 'kv'), may hold values from -0.125 to 0.125
- up_weight: bfloat16 [2048, 8192], P('seq', 'kv'), may hold values from -0.125 to 0.125
- down_weight: bfloat16 [8192, 2048], P(('kv', 'seq')), may hold values from -0.0625 to 0.0625
- cotangent: bfloat16 [1, 4096, 2048], P(None, 'seq'), may hold values from -6 to 6
Outputs:
- activations: bfloat16 [1, 4096, 2048], P(None, 'seq')
- grad_tokens: float32 [1, 4096, 2048], P(None, 'seq')
- grad_g_attn: float32 [2048], P('seq')
- grad_w_query: float32 [2048, 2048], P('seq', 'kv')
- grad_w_kv: float32 [2, 2048, 512], P(None, 'seq', 'kv')
- grad_w_out: float32 [2048, 2048], P(('kv', 'seq'))
- grad_lora_down: float32 [3, 2048, 8], P(None, 'seq')
- grad_lora_up_query: float32 [8, 2048], P(None, ('kv', 'seq'))
- grad_lora_up_kv: float32 [2, 8, 512], P(None, None, ('kv', 'seq'))
- grad_lora_down_out: float32 [2048, 8], P(('kv', 'seq'))
- grad_lora_up_out: float32 [8, 2048], P(None, 'seq')
- grad_fmap_query: float32 [32, 64, 64], P('kv', 'seq')
- grad_fmap_key: float32 [8, 64, 64], P('kv', 'seq')
- grad_g_mlp: float32 [2048], P('seq')
- grad_w_gate: float32 [2048, 8192], P('seq', 'kv')
- grad_w_up: float32 [2048, 8192], P('seq', 'kv')
- grad_w_down: float32 [8192, 2048], P(('kv', 'seq'))
The draws below stay inside these ranges and needn't reach their ends.
All inputs are finite; a program needn't handle non-finite values.
Results may differ from the reference program's by a relative error of at most 0.024.
Values may be sent and summed in bfloat16 or wider, within the bound.
No kernel may reach another device: no remote copies, remote signals or barrier semaphores. Data moves between devices by JAX's collectives and lax.ppermute only.
A program may use at most 256 MiB of HBM per device.

```python
import jax
import jax.numpy as jnp
from jax import lax

MODEL_WIDTH = 2048
FF = 8192
QUERY_HEADS = 32
KEY_VALUE_HEADS = 8
HEAD_WIDTH = 64
ADAPTER_RANK = 8
WIN = 64
SPAN = 512
SEQS = 1
LENGTH = 4096
N_SEQ = 8


def level_of(key, dims, split, least, high):
    level, own = 1.0, jax.random.fold_in(key, 6)
    for dim, parts in split:
        heights = jnp.exp(jax.random.uniform(jax.random.fold_in(own, dim), (parts,), jnp.float32, least / len(split), high / len(split)))
        level = level * jnp.repeat(heights, dims[dim] // parts).reshape([-1 if axis == dim else 1 for axis in range(len(dims))])
    return level


def bell_draw(key, shape, scale, bound, split=(), held_as=jnp.bfloat16):
    drawn = scale * jax.random.normal(key, shape, jnp.float32)
    if split:
        drawn = drawn * level_of(key, shape, split, -0.22, 0.18)
    return jnp.clip(drawn, -bound, bound).astype(held_as)


def setup_inputs(seed: int = 0) -> dict:
    keys = jax.random.split(jax.random.key(seed), 18)
    tokens = bell_draw(keys[0], (SEQS, LENGTH, MODEL_WIDTH), 1.0, 6.0, ((1, 8),))
    attention_norm_gain = jnp.clip(1.0 + 0.1 * jax.random.normal(keys[1], (MODEL_WIDTH,), jnp.float32), 0.5, 1.5).astype(jnp.bfloat16)
    query_weight = bell_draw(keys[2], (MODEL_WIDTH, QUERY_HEADS * HEAD_WIDTH), MODEL_WIDTH ** -0.5, 0.125, ((0, 8), (1, 4)))
    key_value_weight = bell_draw(keys[3], (2, MODEL_WIDTH, KEY_VALUE_HEADS * HEAD_WIDTH), MODEL_WIDTH ** -0.5, 0.125, ((1, 8), (2, 4)))
    output_weight = bell_draw(keys[4], (QUERY_HEADS * HEAD_WIDTH, MODEL_WIDTH), (QUERY_HEADS * HEAD_WIDTH // 16) ** -0.5, 0.5, ((0, 32),))
    adapter_down_matrices = bell_draw(keys[5], (3, MODEL_WIDTH, ADAPTER_RANK), MODEL_WIDTH ** -0.5, 0.125, ((1, 8),))
    adapter_query_up = bell_draw(keys[6], (ADAPTER_RANK, QUERY_HEADS * HEAD_WIDTH), ADAPTER_RANK ** -0.5, 2.0, ((1, 32),))
    adapter_key_value_up = bell_draw(keys[7], (2, ADAPTER_RANK, KEY_VALUE_HEADS * HEAD_WIDTH), ADAPTER_RANK ** -0.5, 2.0, ((2, 32),))
    adapter_output_down = bell_draw(keys[8], (QUERY_HEADS * HEAD_WIDTH, ADAPTER_RANK), (QUERY_HEADS * HEAD_WIDTH // 16) ** -0.5, 0.5, ((0, 32),))
    adapter_output_up = bell_draw(keys[9], (ADAPTER_RANK, MODEL_WIDTH), ADAPTER_RANK ** -0.5, 2.0, ((1, 8),))
    query_feature_matrix = bell_draw(keys[10], (QUERY_HEADS, HEAD_WIDTH, HEAD_WIDTH), (HEAD_WIDTH // 2) ** -0.5, 1.0, ((0, 4), (1, 8)))
    key_feature_matrix = bell_draw(keys[11], (KEY_VALUE_HEADS, HEAD_WIDTH, HEAD_WIDTH), (HEAD_WIDTH // 2) ** -0.5, 1.0, ((0, 4), (1, 8)))
    feedforward_norm_gain = jnp.clip(1.0 + 0.1 * jax.random.normal(keys[12], (MODEL_WIDTH,), jnp.float32), 0.5, 1.5).astype(jnp.bfloat16)
    gate_weight = bell_draw(keys[13], (MODEL_WIDTH, FF), MODEL_WIDTH ** -0.5, 0.125, ((0, 8), (1, 4)))
    up_weight = bell_draw(keys[14], (MODEL_WIDTH, FF), MODEL_WIDTH ** -0.5, 0.125, ((0, 8), (1, 4)))
    down_weight = bell_draw(keys[15], (FF, MODEL_WIDTH), FF ** -0.5, 0.0625, ((0, 32),))
    cotangent = bell_draw(keys[16], (SEQS, LENGTH, MODEL_WIDTH), 1.0, 6.0, ((1, 8),))
    return dict(tokens=tokens, attention_norm_gain=attention_norm_gain, query_weight=query_weight, key_value_weight=key_value_weight, output_weight=output_weight, adapter_down_matrices=adapter_down_matrices, adapter_query_up=adapter_query_up, adapter_key_value_up=adapter_key_value_up, adapter_output_down=adapter_output_down, adapter_output_up=adapter_output_up, query_feature_matrix=query_feature_matrix, key_feature_matrix=key_feature_matrix, feedforward_norm_gain=feedforward_norm_gain, gate_weight=gate_weight, up_weight=up_weight, down_weight=down_weight, cotangent=cotangent)


highest_precision = lax.Precision.HIGHEST
epsilon = 1e-05

@jax.custom_vjp
def low(v):
    return lax.optimization_barrier(v.astype(jnp.bfloat16)).astype(jnp.float32)

@jax.custom_vjp
def lowrank_backward(v):
    return v

def low_keep(v):
    return (low(v), None)

def low_pass(kept, grad):
    return (grad,)

def back_keep(v):
    return (v, None)

def back_low(kept, grad):
    return (low(grad),)
low.defvjp(low_keep, low_pass)
lowrank_backward.defvjp(back_keep, back_low)

def rounded_values(value):
    return low(lowrank_backward(value))

def rms_norm(values, gain):
    scale = lax.rsqrt(lax.optimization_barrier(jnp.mean(values * values, -1, keepdims=True)) + epsilon)
    return values * scale * gain

def features(input_tokens, fmap):
    mixing = lowrank_backward(jnp.einsum('...hd,hde->...he', input_tokens, fmap, precision=highest_precision))
    return rounded_values(jnp.concatenate([jax.nn.softmax(mixing, -1), jax.nn.softmax(-mixing, -1)], -1))

def attention(query_rows, key_rows, value_rows, query_feature_matrix, key_feature_matrix):
    sequences = query_rows.shape[0]
    group_size = QUERY_HEADS // KEY_VALUE_HEADS
    score_scale = HEAD_WIDTH ** (-0.5)
    zero_rows = jnp.zeros((sequences, WIN, KEY_VALUE_HEADS, HEAD_WIDTH), jnp.float32)
    key_pad = jnp.concatenate([zero_rows, key_rows], 1)
    value_pad = jnp.concatenate([zero_rows, value_rows], 1)
    row_ids = jnp.arange(SPAN, dtype=jnp.int32)[:, None]
    col_ids = jnp.arange(SPAN + WIN, dtype=jnp.int32)[None, :]
    in_band = (col_ids > row_ids) & (col_ids <= row_ids + WIN)
    is_early = col_ids[:, :SPAN] <= row_ids

    def step(carry, block_index):
        states, normalizer = carry
        offset = (block_index * SPAN).astype(jnp.int32)
        query_block = lax.dynamic_slice_in_dim(query_rows, offset, SPAN, 1)
        key_block = lax.dynamic_slice_in_dim(key_pad, offset, SPAN + WIN, 1)
        value_block = lax.dynamic_slice_in_dim(value_pad, offset, SPAN + WIN, 1)
        is_valid = offset - WIN + jnp.arange(SPAN + WIN, dtype=jnp.int32) >= 0
        query_feat = features(query_block, query_feature_matrix).reshape(sequences, SPAN, KEY_VALUE_HEADS, group_size, 2 * HEAD_WIDTH)
        key_feat = features(key_block[:, :SPAN], key_feature_matrix) * is_valid[None, :SPAN, None, None].astype(jnp.float32)
        query_groups = query_block.reshape(sequences, SPAN, KEY_VALUE_HEADS, group_size, HEAD_WIDTH)
        scores = lowrank_backward(jnp.einsum('sikgd,sjkd->skgij', query_groups, key_block, precision=highest_precision) * score_scale)
        linear = lowrank_backward(jnp.einsum('sikgf,sjkf->skgij', query_feat, key_feat, precision=highest_precision))
        window = jnp.where(in_band & is_valid[None, :], jnp.exp(scores), 0.0)
        earlier = jnp.where(is_early, linear, 0.0)
        numerator = jnp.einsum('skgij,sjkd->sikgd', low(window), value_block, precision=highest_precision)
        numerator = numerator + jnp.einsum('skgij,sjkd->sikgd', low(earlier), value_block[:, :SPAN], precision=highest_precision)
        numerator = lowrank_backward(numerator + jnp.einsum('sikgf,skfd->sikgd', query_feat, low(states), precision=highest_precision))
        denominator = jnp.transpose(lax.optimization_barrier(jnp.sum(window, -1)) + lax.optimization_barrier(jnp.sum(earlier, -1)), (0, 3, 1, 2))
        denominator = denominator + jnp.einsum('sikgf,skf->sikg', query_feat, normalizer, precision=highest_precision)
        result = numerator / denominator[..., None]
        block_total = lowrank_backward(jnp.einsum('sjkf,sjkd->skfd', key_feat, value_block[:, :SPAN], precision=highest_precision))
        return ((states + block_total, normalizer + lax.optimization_barrier(jnp.sum(key_feat, 1))), result)
    initial = (jnp.zeros((sequences, KEY_VALUE_HEADS, 2 * HEAD_WIDTH, HEAD_WIDTH), jnp.float32), jnp.zeros((sequences, KEY_VALUE_HEADS, 2 * HEAD_WIDTH), jnp.float32))
    unused, results = lax.scan(jax.checkpoint(step), initial, jnp.arange(N_SEQ, dtype=jnp.int32))
    results = jnp.transpose(results, (1, 0, 2, 3, 4, 5))
    return results.reshape(sequences, N_SEQ * SPAN, QUERY_HEADS * HEAD_WIDTH)

def forward_block_pass(tokens, attention_norm_gain, query_weight, key_value_weight, output_weight, adapter_down_matrices, adapter_query_up, adapter_key_value_up, adapter_output_down, adapter_output_up, query_feature_matrix, key_feature_matrix, feedforward_norm_gain, gate_weight, up_weight, down_weight):
    sequences = tokens.shape[0]
    normalized_input = low(rms_norm(tokens, attention_norm_gain))
    adapter_token_rows = rounded_values(jnp.einsum('fwg,ogx->ofwx', normalized_input, adapter_down_matrices, precision=highest_precision))
    query_rows = rounded_values(jnp.dot(normalized_input, query_weight, precision=highest_precision) + jnp.dot(adapter_token_rows[0], adapter_query_up, precision=highest_precision))
    key_value_rows = rounded_values(jnp.einsum('zai,hik->hzak', normalized_input, key_value_weight, precision=highest_precision) + jnp.einsum('qafx,qxd->qafd', adapter_token_rows[1:], adapter_key_value_up, precision=highest_precision))
    attended_output = low(attention(query_rows.reshape(sequences, LENGTH, QUERY_HEADS, HEAD_WIDTH), key_value_rows[0].reshape(sequences, LENGTH, KEY_VALUE_HEADS, HEAD_WIDTH), key_value_rows[1].reshape(sequences, LENGTH, KEY_VALUE_HEADS, HEAD_WIDTH), query_feature_matrix, key_feature_matrix))
    adapter_output = rounded_values(jnp.dot(attended_output, adapter_output_down, precision=highest_precision))
    branch_output = lowrank_backward(jnp.dot(attended_output, output_weight, precision=highest_precision) + jnp.dot(adapter_output, adapter_output_up, precision=highest_precision))
    middle_hidden = tokens + branch_output
    normed_two = low(rms_norm(middle_hidden, feedforward_norm_gain))
    gate_pre = lowrank_backward(jnp.dot(normed_two, gate_weight, precision=highest_precision))
    up_pre = lowrank_backward(jnp.dot(normed_two, up_weight, precision=highest_precision))
    hidden = low(jax.nn.silu(gate_pre) * up_pre)
    return middle_hidden + lowrank_backward(jnp.dot(hidden, down_weight, precision=highest_precision))

def reference(tokens, attention_norm_gain, query_weight, key_value_weight, output_weight, adapter_down_matrices, adapter_query_up, adapter_key_value_up, adapter_output_down, adapter_output_up, query_feature_matrix, key_feature_matrix, feedforward_norm_gain, gate_weight, up_weight, down_weight, cotangent):
    input_tokens = (tokens, attention_norm_gain, query_weight, key_value_weight, output_weight, adapter_down_matrices, adapter_query_up, adapter_key_value_up, adapter_output_down, adapter_output_up, query_feature_matrix, key_feature_matrix, feedforward_norm_gain, gate_weight, up_weight, down_weight)
    input_tokens = tuple((item.astype(jnp.float32) for item in input_tokens))
    result, pull = jax.vjp(forward_block_pass, *input_tokens)
    grads = pull(cotangent.astype(jnp.float32))
    return (result.astype(jnp.bfloat16), grads[0], grads[1], grads[2], grads[3], grads[4], grads[5], grads[6], grads[7], grads[8], grads[9], grads[10], grads[11], grads[12], grads[13], grads[14], grads[15])
```

```python
import jax
import jax.numpy as jnp
from jax import lax
from jax.sharding import PartitionSpec as P

WIN = 64
RING = 4
epsilon = 1e-05
bf16 = jnp.bfloat16
f32 = jnp.float32


def trade(array, axis, mask):
    count = lax.axis_size(axis)
    return lax.ppermute(array, axis, [(i, i ^ mask) for i in range(count)])


def moved(array, axis, by):
    count = lax.axis_size(axis)
    pairs = [(i, i + by) for i in range(count) if 0 <= i + by < count]
    return lax.ppermute(array, axis, pairs)


def earlier_sum(part, axis, sign):
    count = lax.axis_size(axis)
    result = None
    window, reach = part, 1
    while reach < count:
        terms = [moved(window, axis, sign * reach * k) for k in (1, 2, 3) if reach * k < count]
        total = terms[0]
        for term in terms[1:]:
            total = total + term
        result = total if result is None else result + total
        window = window + total
        reach *= 4
    return result


def dot(a, b):
    return jnp.dot(a, b, preferred_element_type=f32)


def dot_nt(a, b):
    return lax.dot_general(a, b, (((1,), (1,)), ((), ())), preferred_element_type=f32)


def dot_tn(a, b):
    return lax.dot_general(a, b, (((0,), (0,)), ((), ())), preferred_element_type=f32)


def add_low(a, b):
    return (a.astype(f32) + b.astype(f32)).astype(bf16)


def placed(pieces, order):
    rows = pieces[0].shape[0]
    result = jnp.zeros((rows * len(pieces),) + pieces[0].shape[1:], pieces[0].dtype)
    for piece, at in zip(pieces, order):
        result = lax.dynamic_update_slice_in_dim(result, piece, at * rows, 0)
    return result


def block(array, at, rows, axis=0):
    return lax.dynamic_slice_in_dim(array, at * rows, rows, axis)


def seq_gather(own, pair):
    got = {0: own}
    got[2 * pair] = trade(own, "seq", 2 * pair)
    got[pair] = trade(own, "seq", pair)
    got[3 * pair] = trade(got[2 * pair], "seq", pair)
    bit = 1
    while bit < pair:
        for mask in list(got):
            got[mask | bit] = trade(got[mask], "seq", bit)
        bit *= 2
    return [got[i] for i in range(len(got))]


def token_gather(own, pair):
    got = [own, None, None, None]
    got[2] = trade(own, "seq", 2 * pair)
    got[1] = trade(own, "seq", pair)
    got[3] = trade(got[2], "seq", pair)
    result = []
    for piece in got:
        side = trade(piece, "kv", 2)
        result.append([piece, trade(piece, "kv", 1), side, trade(side, "kv", 1)])
    return result


def token_sum(parts, pair):
    sums = {}
    for d in (3, 2, 1, 0):
        near = add_low(parts[d][0], trade(parts[d][1], "kv", 1))
        side = add_low(parts[d][2], trade(parts[d][3], "kv", 1))
        sums[d] = add_low(near, trade(side, "kv", 2))
    far = add_low(sums[2], trade(sums[3], "seq", pair))
    near = add_low(sums[0], trade(sums[1], "seq", pair))
    return add_low(near, trade(far, "seq", 2 * pair))


def kv_sum(parts):
    near = add_low(parts[0], trade(parts[1], "kv", 1))
    side = add_low(parts[2], trade(parts[3], "kv", 1))
    return near.astype(f32) + trade(side, "kv", 2).astype(f32)


def kv_gather(own):
    side = trade(own, "kv", 2)
    return [own, trade(own, "kv", 1), side, trade(side, "kv", 1)]


def kv_total(own):
    for mask in (1, 2):
        low = lax.optimization_barrier(own.astype(bf16))
        own = low.astype(f32) + trade(low, "kv", mask).astype(f32)
    return own


def seq_scatter(parts, pair):
    parts = list(parts)
    size = len(parts)
    bit = 1
    while bit < pair:
        for i in range(0, size, 2 * bit):
            parts[i] = add_low(parts[i], trade(parts[i + bit], "seq", bit))
        bit *= 2
    far = add_low(parts[2 * pair], trade(parts[3 * pair], "seq", pair))
    near = add_low(parts[0], trade(parts[pair], "seq", pair))
    return near.astype(f32) + trade(far, "seq", 2 * pair).astype(f32)


def seq_halves(parts):
    bit = parts.shape[0] // 2
    while bit:
        parts = add_low(parts[:bit], trade(parts[bit:], "seq", bit))
        bit //= 2
    return parts[0]


def spread_features(mixing):
    return jnp.concatenate([jax.nn.softmax(mixing, -1), jax.nn.softmax(-mixing, -1)], -1)


def feature_map(rows, matrix):
    mixing = jnp.einsum("thd,hde->the", rows, matrix, preferred_element_type=f32)
    return mixing, spread_features(mixing).astype(bf16)


def feature_back(rows, matrix, mixing, grad):
    grad = grad.astype(bf16).astype(f32)
    unused, pull = jax.vjp(spread_features, mixing)
    grad_mix = pull(grad)[0].astype(bf16)
    grad_rows = jnp.einsum("the,hde->thd", grad_mix, matrix, preferred_element_type=f32)
    grad_matrix = jnp.einsum("thd,the->hde", rows, grad_mix, preferred_element_type=f32)
    return grad_rows, grad_matrix


def norm_back(values, scale, gain, grad):
    scaled = grad * gain
    gain_grad = jnp.sum(grad * values * scale, 0)
    mean = jnp.mean(scaled * values, -1, keepdims=True)
    return gain_grad, scale * scaled - values * scale * scale * scale * mean


def inverse_rms(values):
    return lax.rsqrt(jnp.mean(values * values, -1, keepdims=True) + epsilon)


def window_masks(length, offset):
    row_ids = jnp.arange(length)[:, None]
    col_ids = jnp.arange(length + WIN)[None, :]
    is_valid = offset - WIN + jnp.arange(length + WIN) >= 0
    in_window = (col_ids > row_ids) & (col_ids <= row_ids + WIN) & is_valid[None, :]
    is_early = col_ids[:, :length] <= row_ids
    return in_window, is_early, is_valid[:length]


def attend(query, feat, key, value, kfeat, state, norm, masks):
    in_window, is_early = masks
    length = query.shape[0]
    scores = jnp.einsum("ikgd,jkd->kgij", query, key, preferred_element_type=f32) * query.shape[-1] ** (-0.5)
    window = jnp.where(in_window, jnp.exp(scores), 0.0)
    linear = jnp.einsum("ikgf,jkf->kgij", feat, kfeat, preferred_element_type=f32)
    early = jnp.where(is_early, linear, 0.0)
    window_low, early_low = window.astype(bf16), early.astype(bf16)
    top = jnp.einsum("kgij,jkd->ikgd", window_low, value, preferred_element_type=f32)
    top = top + jnp.einsum("kgij,jkd->ikgd", early_low, value[:length], preferred_element_type=f32)
    top = top + jnp.einsum("ikgf,kfd->ikgd", feat, state.astype(bf16), preferred_element_type=f32)
    under = jnp.transpose(jnp.sum(window, -1) + jnp.sum(early, -1), (2, 0, 1))
    under = under + jnp.sum(feat.astype(f32) * norm[None, :, None, :], -1)
    return window_low, early_low, top, under


def attend_state_back(feat, top, under, grad):
    grad_top = (grad / under[..., None]).astype(bf16)
    grad_under = -jnp.sum(grad * top, -1) / (under * under)
    grad_state = jnp.einsum("ikgf,ikgd->kfd", feat, grad_top, preferred_element_type=f32)
    grad_norm = jnp.sum(feat.astype(f32) * grad_under[..., None], (0, 2))
    return grad_top, grad_under, grad_state, grad_norm


def attend_back(query, feat, key, value, kfeat, state, norm, window, early, grad_top, grad_under, is_early):
    length = query.shape[0]
    scale = query.shape[-1] ** (-0.5)
    e = jnp.einsum("ikgd,jkd->kgij", grad_top, value, preferred_element_type=f32)
    e = e + jnp.transpose(grad_under, (1, 2, 0))[..., None]
    grad_window = (e * window.astype(f32)).astype(bf16)
    grad_early = jnp.where(is_early, e[..., :length], 0.0).astype(bf16)
    grad_query = jnp.einsum("kgij,jkd->ikgd", grad_window, key, preferred_element_type=f32) * scale
    grad_key = jnp.einsum("kgij,ikgd->jkd", grad_window, query, preferred_element_type=f32) * scale
    grad_feat = jnp.einsum("kgij,jkf->ikgf", grad_early, kfeat, preferred_element_type=f32)
    grad_feat = grad_feat + jnp.einsum("ikgd,kfd->ikgf", grad_top, state.astype(bf16), preferred_element_type=f32)
    grad_feat = grad_feat + grad_under[..., None] * norm[None, :, None, :]
    grad_kfeat = jnp.einsum("kgij,ikgf->jkf", grad_early, feat, preferred_element_type=f32)
    grad_value = jnp.einsum("kgij,ikgd->jkd", window, grad_top, preferred_element_type=f32)
    from_early = jnp.einsum("kgij,ikgd->jkd", early, grad_top, preferred_element_type=f32)
    grad_value = grad_value + jnp.pad(from_early, ((0, WIN), (0, 0), (0, 0)))
    return grad_query, grad_feat, grad_key, grad_value, grad_kfeat


def per_device(
    tokens,
    attention_norm_gain,
    query_weight,
    key_value_weight,
    output_weight,
    adapter_down_matrices,
    adapter_query_up,
    adapter_key_value_up,
    adapter_output_down,
    adapter_output_up,
    query_feature_matrix,
    key_feature_matrix,
    feedforward_norm_gain,
    gate_weight,
    up_weight,
    down_weight,
    cotangent,
):
    count = lax.axis_size("seq")
    pair = count // RING
    place = lax.axis_index("seq")
    along, beside = place // pair, place % pair
    lane = lax.axis_index("kv")
    kv_count = lax.axis_size("kv")
    unused, length, width = tokens.shape
    chunk = length // kv_count
    depth = query_weight.shape[0]
    q_cols = query_weight.shape[1]
    kv_cols = key_value_weight.shape[2]
    head_size = query_feature_matrix.shape[2]
    heads = query_feature_matrix.shape[0]
    kv_heads = key_feature_matrix.shape[0]
    group = heads // kv_heads
    rank = adapter_query_up.shape[0]
    all_cols = q_cols + 2 * kv_cols
    lora_cols = 3 * rank

    def wide(a, rows, cols):
        return jnp.pad(a, ((0, rows - a.shape[0]), (0, cols - a.shape[1])))

    small_rows = q_cols // count
    fk_rows = kv_heads * (head_size // count)
    up_rows = 2 * rank
    vec = jnp.concatenate(
        [attention_norm_gain[None], feedforward_norm_gain[None], adapter_output_up], 0
    )
    vec_rows = vec.size // 64
    small = jnp.concatenate(
        [
            wide(
                jnp.concatenate(
                    [query_feature_matrix.reshape(small_rows, head_size), adapter_output_down], 1
                ),
                small_rows,
                104,
            ),
            wide(key_feature_matrix.reshape(fk_rows, head_size), fk_rows, 104),
            wide(
                jnp.concatenate(
                    [
                        adapter_key_value_up.reshape(up_rows, -1),
                        wide(adapter_query_up, up_rows, adapter_query_up.shape[1]),
                    ],
                    1,
                ),
                up_rows,
                104,
            ),
            wide(vec.reshape(vec_rows, 64), vec_rows, 104),
        ],
        0,
    )
    packed = jnp.concatenate(
        [
            query_weight,
            key_value_weight[0],
            key_value_weight[1],
            adapter_down_matrices[0],
            adapter_down_matrices[1],
            adapter_down_matrices[2],
            wide(small, depth, 104),
        ],
        1,
    )
    order = [place ^ i for i in range(count)]
    pieces = seq_gather(packed, pair)
    halo = moved(tokens[0, length - WIN :], "seq", 1)

    full = placed(pieces, order)
    small_full = full.reshape(count, depth, -1)[:, :, all_cols + lora_cols :]
    at = small_rows
    fq_w = jnp.transpose(
        small_full[:, :at, :head_size].reshape(count, heads, -1, head_size), (1, 0, 2, 3)
    ).reshape(heads, head_size, head_size)
    out_down = small_full[:, :at, head_size : head_size + rank].reshape(q_cols, rank)
    fk_w = jnp.transpose(
        small_full[:, at : at + fk_rows, :head_size].reshape(count, kv_heads, -1, head_size),
        (1, 0, 2, 3),
    ).reshape(kv_heads, head_size, head_size)
    at += fk_rows
    kv_each = kv_cols // count
    q_each = q_cols // count
    kv_up = jnp.transpose(
        small_full[:, at : at + up_rows, :kv_each].reshape(count, 2, rank, kv_each), (1, 2, 0, 3)
    ).reshape(2, rank, kv_cols)
    q_up = jnp.transpose(
        small_full[:, at : at + rank, kv_each : kv_each + q_each], (1, 0, 2)
    ).reshape(rank, q_cols)
    at += up_rows
    vecs = jnp.transpose(
        small_full[:, at : at + vec_rows, :64].reshape(count, 2 + rank, depth), (1, 0, 2)
    ).reshape(2 + rank, width)
    gain_one = vecs[0].astype(f32)
    gain_two = vecs[1].astype(f32)
    out_up = vecs[2:]
    spare = full.shape[1] - all_cols
    ups = jnp.concatenate(
        [
            jnp.pad(q_up, ((0, 0), (0, 2 * kv_cols))),
            jnp.pad(kv_up[0], ((0, 0), (q_cols, kv_cols))),
            jnp.pad(kv_up[1], ((0, 0), (q_cols + kv_cols, 0))),
            jnp.zeros((spare - lora_cols, all_cols), bf16),
        ],
        0,
    )

    out_pieces = [output_weight, None, None, None]
    out_pieces[2] = trade(output_weight, "seq", 2 * pair)
    out_pieces[1] = trade(output_weight, "seq", pair)
    out_pieces[3] = trade(out_pieces[2], "seq", pair)
    rows_out = output_weight.shape[0]
    units_each = down_weight.shape[0]
    units = gate_weight.shape[1] // RING

    def unit_block(d):
        at = (along ^ d) * units
        return jnp.concatenate(
            [
                lax.dynamic_slice_in_dim(gate_weight, at, units, 1),
                lax.dynamic_slice_in_dim(up_weight, at, units, 1),
            ],
            1,
        )

    gu_pieces = {d * pair: unit_block(d) for d in range(RING)}
    for d in (2, 1, 3):
        gu_pieces[d * pair] = trade(gu_pieces[d * pair], "seq", d * pair)
    mixed = [jnp.concatenate([down_weight] + out_pieces, 0)]
    bit = 1
    while bit < pair:
        for mask in list(gu_pieces):
            gu_pieces[mask | bit] = trade(gu_pieces[mask], "seq", bit)
        mixed = mixed + [trade(m, "seq", bit) for m in mixed]
        bit *= 2
    gu_w = placed([gu_pieces[i] for i in range(count)], order)
    down_w = placed([m[:units_each] for m in mixed], [beside ^ i for i in range(pair)])
    out_w = placed(
        [mixed[i % pair][units_each + (i // pair) * rows_out :][:rows_out] for i in range(count)],
        order,
    )
    out_ext = jnp.concatenate([out_w, wide(out_down, q_cols, 128)], 1)

    own_dy = block(cotangent[0], lane, chunk)
    dy_pieces = token_gather(own_dy, pair)

    extended = jnp.concatenate([halo, tokens[0]], 0).astype(f32)
    scale_ext = inverse_rms(extended)
    normed_ext = (extended * scale_ext * gain_one).astype(bf16)
    normed = normed_ext[WIN:]
    scale_one = scale_ext[WIN:]
    projected = dot(normed_ext, full)
    lora_ext = projected[:, all_cols:].astype(bf16)
    qkv = (projected[:, :all_cols] + dot(lora_ext, ups)).astype(bf16)
    query = qkv[WIN:, :q_cols].reshape(length, heads, head_size)
    key_ext = qkv[:, q_cols : q_cols + kv_cols].reshape(-1, kv_heads, head_size)
    value_ext = qkv[:, q_cols + kv_cols :].reshape(-1, kv_heads, head_size)
    in_window, is_early, is_valid = window_masks(length, place * length)
    key_mask = is_valid[:, None, None]
    key_mix, key_feat = feature_map(key_ext[:length], fk_w)
    key_feat = jnp.where(key_mask, key_feat, jnp.zeros_like(key_feat))
    value_head = value_ext[:length]
    totals = jnp.einsum("jkf,jkd->kfd", key_feat, value_head, preferred_element_type=f32)
    feat_sums = jnp.sum(key_feat.astype(f32), 0)
    both = earlier_sum(
        jnp.concatenate([totals, jnp.pad(feat_sums[..., None], ((0, 0), (0, 0), (0, 63)))], -1), "seq", 1
    )
    states, norms = both[..., :head_size], both[..., head_size]
    query_mix, query_feat = feature_map(query, fq_w)
    query_groups = query.reshape(length, kv_heads, group, head_size)
    feat_groups = query_feat.reshape(length, kv_heads, group, 2 * head_size)
    window, early, top, under = attend(
        query_groups, feat_groups, key_ext, value_ext, key_feat, states, norms, (in_window, is_early)
    )
    attended = (top / under[..., None]).astype(bf16).reshape(length, q_cols)

    nears = [lane ^ k for k in range(kv_count)]
    chunks = [block(attended, k, chunk) for k in nears]
    branch = kv_sum([dot(c, out_ext).astype(bf16) for c in chunks])
    lora_out = branch[:, width : width + rank].astype(bf16)
    own_tokens = block(tokens[0], lane, chunk).astype(f32)
    middle = own_tokens + branch[:, :width] + dot(lora_out, out_up)
    scale_two = inverse_rms(middle)
    normed_two = (middle * scale_two * gain_two).astype(bf16)

    n_pieces = token_gather(normed_two, pair)
    grad_parts = []
    out_parts = []
    n_blocks, dy_blocks, hidden_blocks, gu_blocks = [], [], [], []
    for d in range(RING):
        n_block = jnp.concatenate(n_pieces[d], 0)
        dy_block = jnp.concatenate(dy_pieces[d], 0)
        grad_hidden = dot_nt(dy_block, down_w)
        pre = dot(n_block, gu_w)
        gate, up = pre[:, :units], pre[:, units:]
        sigma = jax.nn.sigmoid(gate)
        activated = gate * sigma
        hidden = (activated * up).astype(bf16)
        grad_gate = (grad_hidden * up * sigma * (1.0 + gate * (1.0 - sigma))).astype(bf16)
        grad_up = (grad_hidden * activated).astype(bf16)
        grad_gu = jnp.concatenate([grad_gate, grad_up], 1)
        grad_n = dot_nt(grad_gu, gu_w).astype(bf16)
        down = dot(hidden, down_w).astype(bf16)
        grad_parts.append([grad_n[k * chunk : (k + 1) * chunk] for k in range(kv_count)])
        out_parts.append([down[k * chunk : (k + 1) * chunk] for k in range(kv_count)])
        n_blocks.append(n_block)
        dy_blocks.append(dy_block)
        hidden_blocks.append(hidden)
        gu_blocks.append(grad_gu)
    grad_n2 = token_sum(grad_parts, pair).astype(f32)
    gain_grad_two, grad_mid_norm = norm_back(middle, scale_two, gain_two, grad_n2)
    grad_middle = own_dy.astype(f32) + grad_mid_norm
    grad_branch = grad_middle.astype(bf16)

    ffn_out = token_sum(out_parts, pair).astype(f32)
    own_out = (middle + ffn_out).astype(bf16)
    output = placed(kv_gather(own_out), nears)[None]

    grad_gu_w = dot_tn(jnp.concatenate(n_blocks, 0), jnp.concatenate(gu_blocks, 0)).astype(bf16)
    grad_down_w = dot_tn(jnp.concatenate(hidden_blocks, 0), jnp.concatenate(dy_blocks, 0)).astype(bf16)
    gu_parts = [block(grad_gu_w, i, depth) for i in order]
    down_parts = [block(grad_down_w, beside ^ i, units_each) for i in range(pair)]
    bit = pair // 2
    while bit:
        for i in range(count):
            if i % pair < bit:
                gu_parts[i] = add_low(gu_parts[i], trade(gu_parts[i + bit], "seq", bit))
        down_parts = [
            add_low(down_parts[i], trade(down_parts[i + bit], "seq", bit)) for i in range(bit)
        ]
        bit //= 2
    grad_w_down = down_parts[0].astype(f32)
    gate_cols = []
    for d in range(RING):
        own_part = gu_parts[d * pair]
        gate_cols.append(own_part if d == 0 else trade(own_part, "seq", d * pair))
    grad_w_gate = jnp.zeros(gate_weight.shape, f32)
    grad_w_up = jnp.zeros(up_weight.shape, f32)
    for d in range(RING):
        at = (along ^ d) * units
        grad_w_gate = lax.dynamic_update_slice_in_dim(grad_w_gate, gate_cols[d][:, :units].astype(f32), at, 1)
        grad_w_up = lax.dynamic_update_slice_in_dim(grad_w_up, gate_cols[d][:, units:].astype(f32), at, 1)

    branch_pieces = kv_gather(grad_branch)
    lora_pieces = [wide(dot_nt(g, out_up).astype(bf16), chunk, 128) for g in branch_pieces]
    grad_attended = placed(
        [dot_nt(jnp.concatenate([g, l], 1), out_ext) for g, l in zip(branch_pieces, lora_pieces)], nears
    )
    chunks_all = jnp.concatenate(chunks, 0)
    branch_all = jnp.concatenate(branch_pieces, 0)
    grad_out_w = dot_tn(chunks_all, branch_all).astype(bf16)
    grad_out_down = dot_tn(chunks_all, jnp.concatenate(lora_pieces, 0))[:, :rank]
    grad_out_up = dot_tn(lora_out, grad_branch)
    out_stack = jnp.stack([block(grad_out_w, i, rows_out) for i in order])
    grad_w_out = seq_halves(out_stack).astype(f32)

    grad_groups = grad_attended.reshape(length, kv_heads, group, head_size)
    grad_top, grad_under, grad_state, grad_norm = attend_state_back(feat_groups, top, under, grad_groups)
    later = earlier_sum(
        jnp.concatenate([grad_state, jnp.pad(grad_norm[..., None], ((0, 0), (0, 0), (0, 63)))], -1), "seq", -1
    )
    grad_query_s, grad_qfeat, grad_key_ext, grad_value_ext, grad_kfeat = attend_back(
        query_groups, feat_groups, key_ext, value_ext, key_feat, states, norms, window, early, grad_top, grad_under, is_early
    )
    later_low = later[..., :head_size].astype(bf16)
    later_norms = later[..., head_size]
    grad_kfeat = (
        grad_kfeat
        + jnp.einsum("kfd,jkd->jkf", later_low, value_head, preferred_element_type=f32)
        + later_norms[None]
    )
    grad_kfeat = jnp.where(key_mask, grad_kfeat, 0.0)
    extra = jnp.einsum("jkf,kfd->jkd", key_feat, later_low, preferred_element_type=f32)
    grad_value_ext = grad_value_ext + jnp.pad(extra, ((0, WIN), (0, 0), (0, 0)))
    key_from_feat, grad_fk = feature_back(key_ext[:length], fk_w, key_mix, grad_kfeat)
    grad_key_ext = grad_key_ext + jnp.pad(key_from_feat, ((0, WIN), (0, 0), (0, 0)))
    query_from_feat, grad_fq = feature_back(
        query, fq_w, query_mix, grad_qfeat.reshape(length, heads, 2 * head_size)
    )
    grad_queries = grad_query_s.reshape(length, heads, head_size) + query_from_feat
    grad_kv_ext = jnp.concatenate(
        [grad_key_ext.reshape(-1, kv_cols), grad_value_ext.reshape(-1, kv_cols)], 1
    )
    returned = moved(grad_kv_ext[:WIN].astype(bf16), "seq", -1).astype(f32)
    grad_kv = grad_kv_ext[WIN:] + jnp.pad(returned, ((length - WIN, 0), (0, 0)))
    grad_qkv = jnp.concatenate([grad_queries.reshape(length, q_cols), grad_kv], 1).astype(bf16)

    lora = lora_ext[WIN:]
    grad_lora = dot_nt(grad_qkv, ups).astype(bf16)
    grad_ext = jnp.concatenate([grad_qkv, grad_lora], 1)
    grad_normed_part = dot_nt(grad_ext, full)
    gain_part = jnp.sum(grad_normed_part * extended[WIN:] * scale_one, 0)
    low_part = grad_normed_part.astype(bf16)
    grad_normed = kv_sum([block(low_part, k, chunk) for k in nears])
    own_scale = block(scale_one, lane, chunk)
    unused_gain, grad_resid = norm_back(own_tokens, own_scale, gain_one, grad_normed)
    own_grad = lax.optimization_barrier((grad_middle + grad_resid).astype(bf16))
    grad_tokens = placed([g.astype(f32) for g in kv_gather(own_grad)], nears)[None]

    grad_qkv_w = dot_tn(normed, grad_qkv).astype(bf16)
    grad_w = seq_scatter([block(grad_qkv_w, i, depth) for i in order], pair)
    grad_w_query = grad_w[:, :q_cols]
    grad_w_kv = jnp.stack([grad_w[:, q_cols : q_cols + kv_cols], grad_w[:, q_cols + kv_cols :]])

    grad_up_all = dot_tn(lora[:, :lora_cols], grad_qkv)
    grad_lora_down = dot_tn(grad_lora, normed)[:lora_cols]
    fq_part = jnp.transpose(
        grad_fq.reshape(heads, count, -1, head_size), (1, 0, 2, 3)
    ).reshape(count, small_rows, head_size)
    down_part = grad_out_down.reshape(count, small_rows, rank)
    fk_part = jnp.transpose(
        grad_fk.reshape(kv_heads, count, -1, head_size), (1, 0, 2, 3)
    ).reshape(count, fk_rows, head_size)
    kv_up_part = jnp.transpose(
        jnp.stack(
            [
                grad_up_all[rank : 2 * rank, q_cols : q_cols + kv_cols],
                grad_up_all[2 * rank :, q_cols + kv_cols :],
            ]
        ).reshape(2, rank, count, kv_each),
        (2, 0, 1, 3),
    ).reshape(count, up_rows, kv_each)
    q_up_part = jnp.transpose(grad_up_all[:rank, :q_cols].reshape(rank, count, q_each), (1, 0, 2))
    vec_part = jnp.concatenate(
        [grad_lora_down, grad_out_up, gain_grad_two[None], gain_part[None]], 0
    )
    vec_count = vec_part.shape[0]
    vec_part = jnp.transpose(vec_part.reshape(vec_count, count, depth), (1, 0, 2)).reshape(
        count, -1, 64
    )
    more_rows = vec_part.shape[1]

    def lanes(a):
        return jnp.pad(a, ((0, 0), (0, 0), (0, 128 - a.shape[2])))

    small_part = jnp.concatenate(
        [
            lanes(jnp.concatenate([fq_part, down_part], 2)),
            lanes(fk_part),
            lanes(jnp.concatenate([kv_up_part, jnp.pad(q_up_part, ((0, 0), (0, rank), (0, 0)))], 2)),
            lanes(vec_part),
        ],
        1,
    ).astype(bf16)
    small_part = jnp.take(small_part, jnp.stack(order), 0)
    small_sum = seq_halves(small_part).astype(f32)
    at = small_rows
    grad_fmap_query = small_sum[:at, :head_size].reshape(query_feature_matrix.shape)
    grad_lora_down_out = small_sum[:at, head_size : head_size + rank]
    grad_fmap_key = small_sum[at : at + fk_rows, :head_size].reshape(key_feature_matrix.shape)
    at += fk_rows
    grad_lora_up_kv = small_sum[at : at + up_rows, :kv_each].reshape(2, rank, kv_each)
    grad_lora_up_query = small_sum[at : at + rank, kv_each : kv_each + q_each]
    at += up_rows
    vec_sum = kv_total(small_sum[at : at + more_rows, :64]).reshape(vec_count, depth)
    grad_lora_down = jnp.transpose(vec_sum[:lora_cols].reshape(3, rank, depth), (0, 2, 1))
    grad_lora_up_out = vec_sum[lora_cols : lora_cols + rank]
    grad_g_mlp = vec_sum[lora_cols + rank]
    grad_g_attn = vec_sum[lora_cols + rank + 1]
    return (
        output,
        grad_tokens,
        grad_g_attn,
        grad_w_query,
        grad_w_kv,
        grad_w_out,
        grad_lora_down,
        grad_lora_up_query,
        grad_lora_up_kv,
        grad_lora_down_out,
        grad_lora_up_out,
        grad_fmap_query,
        grad_fmap_key,
        grad_g_mlp,
        grad_w_gate,
        grad_w_up,
        grad_w_down,
    )


def solution(mesh):
    return jax.shard_map(
        per_device,
        mesh=mesh,
        in_specs=(
            P(None, "seq", None),
            P("seq"),
            P("seq", "kv"),
            P(None, "seq", "kv"),
            P(("kv", "seq"), None),
            P(None, "seq", None),
            P(None, ("kv", "seq")),
            P(None, None, ("kv", "seq")),
            P(("kv", "seq"), None),
            P(None, "seq"),
            P("kv", "seq", None),
            P("kv", "seq", None),
            P("seq"),
            P("seq", "kv"),
            P("seq", "kv"),
            P(("kv", "seq"), None),
            P(None, "seq", None),
        ),
        out_specs=(
            P(None, "seq", None),
            P(None, "seq", None),
            P("seq"),
            P("seq", "kv"),
            P(None, "seq", "kv"),
            P(("kv", "seq"), None),
            P(None, "seq", None),
            P(None, ("kv", "seq")),
            P(None, None, ("kv", "seq")),
            P(("kv", "seq"), None),
            P(None, "seq"),
            P("kv", "seq", None),
            P("kv", "seq", None),
            P("seq"),
            P("seq", "kv"),
            P("seq", "kv"),
            P(("kv", "seq"), None),
        ),
        check_vma=False,
    )
```

```python
import functools

import jax
import jax.numpy as jnp
from jax import lax
from jax.experimental import pallas as pl
from jax.experimental.pallas import tpu as pltpu
from jax.sharding import Mesh, PartitionSpec as P

WIN = 64
RING = 4
SEQ = ("ring", "pair")
STEP = 128
SMALL = 80
LANES = 128
epsilon = 1e-05
bf16 = jnp.bfloat16
f32 = jnp.float32
shape = jax.ShapeDtypeStruct


def trade(array, axis, mask):
    count = lax.axis_size(axis)
    return lax.ppermute(array, axis, [(i, i ^ mask) for i in range(count)])


def moved(array, axis, by):
    count = lax.axis_size(axis)
    pairs = [(i, i + by) for i in range(count) if 0 <= i + by < count]
    return lax.ppermute(array, axis, pairs)


def after(value, *earlier):
    return lax.optimization_barrier((value,) + earlier)[0]


def dot(a, b):
    return jnp.dot(a, b, preferred_element_type=f32)


def dot_nt(a, b):
    return lax.dot_general(a, b, (((1,), (1,)), ((), ())), preferred_element_type=f32)


def dot_tn(a, b):
    return lax.dot_general(a, b, (((0,), (0,)), ((), ())), preferred_element_type=f32)


def add_low(a, b):
    return (a.astype(f32) + b.astype(f32)).astype(bf16)


def block(array, at, rows, axis=0):
    return lax.dynamic_slice_in_dim(array, at * rows, rows, axis)


def own_call(body, outs, inputs, scalars=0, scratch=(), flops=0, room=8, deps=(), hbm=0):
    count, deps = len(inputs), list(deps)

    def run(*refs):
        body(*refs[:count], *refs[count + len(deps) :])

    vmem = pl.BlockSpec(memory_space=pltpu.VMEM)
    smem = pl.BlockSpec(memory_space=pltpu.SMEM)
    size = sum(a.size * a.dtype.itemsize for a in list(inputs)[: count - hbm] + list(outs))
    return pl.pallas_call(
        run,
        out_shape=tuple(outs),
        in_specs=[smem] * scalars
        + [vmem] * (count - scalars - hbm)
        + [pl.BlockSpec(memory_space=pl.ANY)] * (hbm + len(deps)),
        out_specs=tuple(vmem for _ in outs),
        scratch_shapes=list(scratch),
        compiler_params=pltpu.CompilerParams(vmem_limit_bytes=size + room * 2**20),
        cost_estimate=pl.CostEstimate(flops=flops, bytes_accessed=0, transcendentals=0),
    )(*inputs, *deps)


def placed(pieces, rows, order, extra=None, outs=(), more=(), deps=()):
    count = len(pieces)

    def body(order_ref, *refs):
        refs = refs[: count + len(more)] + refs[count + len(more) + len(deps) :]
        out, sems = refs[count + len(more)], refs[-1]
        copies = []
        i = 0
        for piece in refs[:count]:
            for inner in range(0, piece.shape[0], rows):
                at = pl.multiple_of(order_ref[i] * rows, rows)
                copies.append(
                    pltpu.make_async_copy(piece.at[pl.ds(inner, rows)], out.at[pl.ds(at, rows)], sems.at[i])
                )
                copies[-1].start()
                i += 1
        for copy in copies:
            copy.wait()
        if extra is not None:
            extra(out, *refs[count : count + len(more)], *refs[count + len(more) + 1 : -1])

    vmem = pl.BlockSpec(memory_space=pltpu.VMEM)
    total = sum(p.shape[0] for p in pieces)
    result = pl.pallas_call(
        body,
        out_shape=(shape((total, pieces[0].shape[1]), pieces[0].dtype),) + tuple(outs),
        in_specs=[pl.BlockSpec(memory_space=pltpu.SMEM)]
        + [pl.BlockSpec(memory_space=pl.ANY)] * count
        + [vmem] * len(more)
        + [pl.BlockSpec(memory_space=pl.ANY)] * len(deps),
        out_specs=(vmem,) * (1 + len(outs)),
        scratch_shapes=[pltpu.SemaphoreType.DMA((total // rows,))],
        compiler_params=pltpu.CompilerParams(vmem_limit_bytes=16 * 2**20),
        cost_estimate=pl.CostEstimate(flops=0, bytes_accessed=0, transcendentals=0),
    )(jnp.stack(order).astype(jnp.int32), *pieces, *more, *deps)
    return result if outs else result[0]


def rows_placed(order_ref, *refs):
    out = refs[-1]
    each = STEP
    at = 0
    for ref in refs[:-1]:
        for inner in range(0, ref.shape[0], each):
            to = pl.multiple_of(order_ref[at] * each, each)
            out[pl.ds(to, each)] = ref[inner : inner + each].astype(out.dtype)
            at += 1


def pack_weights(*refs):
    q_hbm, kv_hbm = refs[:2]
    number = (len(refs) - 4) // 2
    out_ref, held, sems = refs[2 + number], refs[3 + number : -1], refs[-1]
    depth, q_cols = q_hbm.shape
    kv_cols = kv_hbm.shape[2]
    moves = [(q_hbm, out_ref.at[:, :q_cols])]
    for c in range(2):
        moves.append((kv_hbm.at[c], out_ref.at[:, pl.ds(q_cols + c * kv_cols, kv_cols)]))
    moves += list(zip(refs[2 : 2 + number], held))
    copies = [pltpu.make_async_copy(a, b, sems.at[i]) for i, (a, b) in enumerate(moves)]
    for copy in copies:
        copy.start()
    for copy in copies:
        copy.wait()
    down_ref, fq_ref, outd_ref, fk_ref, kvup_ref, qup_ref, gain_ref, outu_ref = held
    lora = down_ref.shape[0] * down_ref.shape[1]
    rank = down_ref.shape[1]
    size = fq_ref.shape[1]

    def wide(value, rows, cols):
        value = value.astype(f32)
        if value.shape[1] < cols:
            value = jnp.concatenate([value, jnp.zeros((value.shape[0], cols - value.shape[1]), f32)], 1)
        if value.shape[0] < rows:
            value = jnp.concatenate([value, jnp.zeros((rows - value.shape[0], cols), f32)], 0)
        return value

    downs = [wide(down_ref[c], rank, depth) for c in range(down_ref.shape[0])]
    gap = jnp.zeros((size, depth), f32)
    outd = wide(outd_ref[...], rank, depth)
    rest = jnp.zeros((LANES - lora - size - rank, depth), f32)
    tall = jnp.concatenate(downs + [gap, outd, rest], 0)
    groups = [
        wide(fq_ref[...], fq_ref.shape[0], SMALL),
        wide(fk_ref[...], 16, SMALL),
        wide(jnp.concatenate([kvup_ref[...].astype(f32), wide(qup_ref[...], 2 * rank, qup_ref.shape[1])], 1), 16, SMALL),
    ]
    vec = jnp.concatenate(
        [gain_ref[...].astype(f32), outu_ref[...].astype(f32)], 0
    )
    for at in range(0, depth, 64):
        groups.append(wide(vec[:, at : at + 64], 16, SMALL))
    small = wide(jnp.concatenate(groups, 0), depth, SMALL)
    small = jnp.concatenate(
        [jnp.zeros((depth, lora), f32), small, jnp.zeros((depth, LANES - lora - SMALL), f32)], 1
    )
    out_ref[:, q_cols + 2 * kv_cols :] = (tall.T + small).astype(bf16)


def unpack_weights(full_ref, fq_ref, fk_ref, ups_ref, outd_ref, vec_ref, *, count):
    depth = full_ref.shape[0] // count
    all_cols = full_ref.shape[1] - LANES
    heads, size = fq_ref.shape[0], fq_ref.shape[2]
    kv_heads = fk_ref.shape[0]
    rank = vec_ref.shape[0] - 8
    each = size // count
    lora = 3 * rank
    q_cols = heads * size
    kv_cols = kv_heads * size
    q_each, kv_each = q_cols // count, kv_cols // count
    fq_rows = heads * each
    ups_ref[...] = jnp.zeros_like(ups_ref)
    outd_ref[...] = jnp.zeros_like(outd_ref)
    vec_ref[...] = jnp.zeros_like(vec_ref)
    for s in range(count):
        part = full_ref[s * depth : (s + 1) * depth, all_cols:].astype(f32)
        small = part[:, lora : lora + SMALL]
        for h in range(heads):
            fq_ref[h, s * each : (s + 1) * each] = small[h * each : (h + 1) * each, :size]
        outd_ref[s * fq_rows : (s + 1) * fq_rows, :rank] = small[:fq_rows, size : size + rank]
        at = fq_rows
        for h in range(kv_heads):
            fk_ref[h, s * each : (s + 1) * each] = small[at + h * each : at + (h + 1) * each, :size]
        at += 16
        ups_ref[:rank, s * q_each : (s + 1) * q_each] = small[at : at + rank, kv_each : kv_each + q_each]
        for c in range(2):
            to = q_cols + c * kv_cols + s * kv_each
            ups_ref[(c + 1) * rank : (c + 2) * rank, to : to + kv_each] = small[
                at + c * rank : at + (c + 1) * rank, :kv_each
            ]
        at += 16
        for q in range(depth // 64):
            to = s * depth + q * 64
            vec_ref[:, to : to + 64] = small[at : at + 16, :64]
            at += 16


def cut_units(at_ref, gate_ref, up_ref, *outs):
    units = outs[0].shape[1] // 2
    for i, out in enumerate(outs):
        at = pl.multiple_of(at_ref[i] * units, units)
        out[:, :units] = gate_ref[:, pl.ds(at, units)]
        out[:, units:] = up_ref[:, pl.ds(at, units)]


def place_units(at_ref, *refs):
    gate_ref, up_ref = refs[-2:]
    units = refs[0].shape[1] // 2
    for i, ref in enumerate(refs[:-2]):
        at = pl.multiple_of(at_ref[i] * units, units)
        gate_ref[:, pl.ds(at, units)] = ref[:, :units].astype(f32)
        up_ref[:, pl.ds(at, units)] = ref[:, units:].astype(f32)


def softmax_pair(mixing):
    up = jnp.exp(mixing - jnp.max(mixing, -1, keepdims=True))
    down = jnp.exp(jnp.min(mixing, -1, keepdims=True) - mixing)
    up = up / jnp.sum(up, -1, keepdims=True)
    down = down / jnp.sum(down, -1, keepdims=True)
    return jnp.concatenate([up, down], -1).astype(bf16)


def softmax_pair_back(feat, grad):
    size = feat.shape[1] // 2
    feat = feat.astype(f32)
    term = feat * grad.astype(bf16).astype(f32)
    is_up = lax.broadcasted_iota(jnp.int32, term.shape, 1) < size
    up_sum = jnp.sum(jnp.where(is_up, term, 0.0), -1, keepdims=True)
    down_sum = jnp.sum(jnp.where(is_up, 0.0, term), -1, keepdims=True)
    term = term - feat * jnp.where(is_up, up_sum, down_sum)
    return (term[:, :size] - term[:, size:]).astype(bf16)


def with_ones(values, ones):
    rows, size = values.shape
    column = lax.broadcasted_iota(jnp.int32, (rows, size), 1)
    return jnp.concatenate([values, jnp.where(column < ones, 1.0, 0.0).astype(values.dtype)], 1)


def split_column(wide, size):
    column = lax.broadcasted_iota(jnp.int32, wide.shape, 1)
    total = wide[:, size : size + 1]
    high = total.astype(bf16).astype(f32)
    wide = jnp.where(column == size, high, wide)
    return jnp.where(column == size + 1, total - high, wide).astype(bf16)


def inverse_rms(values):
    return lax.rsqrt(jnp.mean(values * values, -1, keepdims=True) + epsilon)


def project(
    place_ref, halo_ref, tokens_ref, full_ref, vec_ref, ups_ref, fk_ref,
    normed_ref, lora_ref, query_ref, kv_ref, feat_ref, total_ref, *, size
):
    length = tokens_ref.shape[0]
    all_cols = ups_ref.shape[1]
    q_cols = query_ref.shape[1]
    gain = vec_ref[0:1]
    ups = ups_ref[...].astype(bf16)
    step = 192
    for at in range(0, length + WIN, step):
        if at == 0:
            rows = jnp.concatenate([halo_ref[...], tokens_ref[: step - WIN]], 0).astype(f32)
        else:
            rows = tokens_ref[at - WIN : at - WIN + step].astype(f32)
        normed = (rows * inverse_rms(rows) * gain).astype(bf16)
        wide = dot(normed, full_ref[...])
        lora = wide[:, all_cols:].astype(bf16)
        qkv = (wide[:, :all_cols] + dot(lora, ups)).astype(bf16)
        kv_ref[at : at + step] = qkv[:, q_cols:]
        skip = WIN if at == 0 else 0
        to = slice(at - WIN + skip, at - WIN + step)
        normed_ref[to] = normed[skip:]
        lora_ref[to] = lora[skip:]
        query_ref[to] = qkv[skip:, :q_cols]
    heads = fk_ref.shape[0]
    hidden = jnp.where(place_ref[0] == 0, WIN, 0)
    valid = lax.broadcasted_iota(jnp.int32, (length, 2 * size), 0) >= hidden
    for k in range(heads):
        keys = kv_ref[:length, k * size : (k + 1) * size]
        values = kv_ref[:length, (heads + k) * size : (heads + k + 1) * size]
        feat = softmax_pair(dot(keys, fk_ref[k].astype(bf16)))
        feat = jnp.where(valid, feat.astype(f32), 0.0).astype(bf16)
        feat_ref[:, k * 2 * size : (k + 1) * 2 * size] = feat
        total_ref[k] = dot_tn(feat, with_ones(values, 1))


def window_mask(step):
    row = lax.broadcasted_iota(jnp.int32, (step, step + WIN), 0)
    col = lax.broadcasted_iota(jnp.int32, (step, step + WIN), 1)
    return (col > row) & (col <= row + WIN), col


def early_mask(rows, cols):
    row = lax.broadcasted_iota(jnp.int32, (rows, cols), 0)
    col = lax.broadcasted_iota(jnp.int32, (rows, cols), 1)
    return col <= row + (cols - rows)


def local_attention(place_ref, q_ref, kv_ref, fq_ref, kfeat_ref, *outs, size):
    kv_heads = kfeat_ref.shape[1] // (2 * size)
    group = fq_ref.shape[0] // kv_heads
    length = kfeat_ref.shape[0]
    step = STEP
    hidden = jnp.where(place_ref[0] == 0, WIN, 0)
    in_window, col = window_mask(step)
    for k in range(kv_heads):
        acc_ref, feat_ref = outs[k], outs[kv_heads + k]
        keys = kv_ref[:, k * size : (k + 1) * size]
        values = with_ones(kv_ref[:, (kv_heads + k) * size : (kv_heads + k + 1) * size], 1)
        kfeat = kfeat_ref[:, k * 2 * size : (k + 1) * 2 * size]
        for g in range(group):
            h = k * group + g
            query = q_ref[:, h * size : (h + 1) * size]
            feat = softmax_pair(dot(query, fq_ref[h].astype(bf16)))
            feat_ref[:, g * 2 * size : (g + 1) * 2 * size] = feat
            query = (query.astype(f32) * size ** (-0.5)).astype(bf16)
            for at in range(0, length, step):
                end = at + step
                mask = in_window & (col >= hidden) if at == 0 else in_window
                weight = jnp.where(mask, jnp.exp(dot_nt(query[at:end], keys[at : end + WIN])), 0.0)
                linear = dot_nt(feat[at:end], kfeat[:end])
                linear = jnp.where(early_mask(step, end), linear, 0.0)
                acc = dot(weight.astype(bf16), values[at : end + WIN])
                acc = acc + dot(linear.astype(bf16), values[:end])
                acc_ref[at:end, g * 2 * size : (g + 1) * 2 * size] = acc


def finish_attention(
    lane_ref, *refs, size, kv_heads
):
    accs, feats = refs[:kv_heads], refs[kv_heads : 2 * kv_heads]
    state_ref, out_w_ref, down_ref = refs[2 * kv_heads : 2 * kv_heads + 3]
    total_ref, out_ref, keep_ref, send_ref = refs[2 * kv_heads + 3 :]
    group = accs[0].shape[1] // (2 * size)
    for k in range(kv_heads):
        state = split_column(state_ref[k], size)
        for g in range(group):
            cols = slice(g * 2 * size, (g + 1) * 2 * size)
            h = k * group + g
            acc = accs[k][:, cols] + dot(feats[k][:, cols], state)
            total_ref[:, h * 2 * size : (h + 1) * 2 * size] = acc
            under = acc[:, size : size + 1] + acc[:, size + 1 : size + 2]
            out_ref[:, h * size : (h + 1) * size] = (acc[:, :size] / under).astype(bf16)
    chunk = keep_ref.shape[0] // 2
    for ref, masks in ((send_ref, (1, 3)), (keep_ref, (0, 2))):
        rows = [out_ref[pl.ds(pl.multiple_of(jnp.bitwise_xor(lane_ref[0], m) * chunk, chunk), chunk)] for m in masks]
        rows = jnp.concatenate(rows, 0)
        width = out_w_ref.shape[1]
        ref[:, :width] = dot(rows, out_w_ref[...]).astype(bf16)
        ref[:, width:] = dot(rows, down_ref[...].astype(bf16)).astype(bf16)


def residual_norm(near_ref, got_ref, tokens_ref, vec_ref, middle_ref, normed_ref, lora_ref):
    width = tokens_ref.shape[1]
    branch = near_ref[...].astype(f32) + got_ref[...].astype(f32)
    rank = vec_ref.shape[0] - 8
    lora = branch[:, width:].astype(bf16)
    lora_ref[...] = lora
    ups = vec_ref[2 : 2 + rank].astype(bf16)
    middle = tokens_ref[...].astype(f32) + branch[:, :width] + dot(lora[:, :rank], ups)
    middle_ref[...] = middle
    normed_ref[...] = (middle * inverse_rms(middle) * vec_ref[1:2]).astype(bf16)


def residual_norm_back(
    near_ref, one_ref, two_ref, three_ref, middle_ref, vec_ref, dy_ref, lora_ref,
    grad_ref, branch_ref, gain_ref, up_ref
):
    grad = near_ref[...].astype(f32) + one_ref[...].astype(f32)
    grad = grad + (two_ref[...].astype(f32) + three_ref[...].astype(f32))
    middle = middle_ref[...]
    scale = inverse_rms(middle)
    rank = vec_ref.shape[0] - 8
    gain_ref[...] = jnp.broadcast_to(jnp.sum(grad * middle * scale, 0, keepdims=True), gain_ref.shape)
    scaled = grad * vec_ref[1:2]
    mean = jnp.mean(scaled * middle, -1, keepdims=True)
    total = dy_ref[...].astype(f32) + scale * scaled - middle * (scale * scale * scale * mean)
    grad_ref[...] = total
    low = total.astype(bf16)
    branch_ref[...] = low
    up_ref[...] = dot_tn(lora_ref[...], low)[:rank]


def attended_back(
    lane_ref, own_ref, side_ref, cross_ref, far_ref, out_w_ref, down_ref, vec_ref, total_ref, *refs, size, kv_heads
):
    feats = refs[:kv_heads]
    tops = refs[kv_heads : 2 * kv_heads]
    state_ref, rows_ref, grad_ref = refs[2 * kv_heads :]
    width = own_ref.shape[1]
    rank = vec_ref.shape[0] - 8
    chunk = own_ref.shape[0]
    ups = vec_ref[2 : 2 + rank].astype(bf16)
    for pieces, masks in (((own_ref, side_ref), (0, 2)), ((cross_ref, far_ref), (1, 3))):
        rows = jnp.concatenate([r[...] for r in pieces], 0)
        lora = dot_nt(rows, ups).astype(bf16)
        lora = jnp.concatenate([lora.astype(f32), jnp.zeros((2 * chunk, LANES - rank), f32)], 1).astype(bf16)
        wide = jnp.concatenate([rows, lora], 1)
        grad = dot_nt(rows, out_w_ref[...]) + dot_nt(lora, down_ref[...].astype(bf16))
        for i, m in enumerate(masks):
            to = pl.ds(pl.multiple_of(jnp.bitwise_xor(lane_ref[0], m) * chunk, chunk), chunk)
            rows_ref[to] = wide[i * chunk : (i + 1) * chunk]
            grad_ref[to] = grad[i * chunk : (i + 1) * chunk]
    group = feats[0].shape[1] // (2 * size)
    for k in range(kv_heads):
        state = None
        for g in range(group):
            h = k * group + g
            cols = slice(g * 2 * size, (g + 1) * 2 * size)
            total = total_ref[:, h * 2 * size : (h + 1) * 2 * size]
            under = total[:, size : size + 1] + total[:, size + 1 : size + 2]
            grad = grad_ref[:, h * size : (h + 1) * size] / under
            grad_under = -jnp.sum(grad * total[:, :size], -1, keepdims=True) / under
            wide = jnp.concatenate([grad, jnp.broadcast_to(grad_under, grad.shape)], 1)
            column = lax.broadcasted_iota(jnp.int32, wide.shape, 1)
            wide = split_column(jnp.where(column > size, 0.0, wide), size)
            tops[k][:, cols] = wide
            term = dot_tn(feats[k][:, cols], wide)
            state = term if state is None else state + term
        state_ref[k] = state


def local_back(
    place_ref, q_ref, kv_ref, fq_ref, kfeat_ref, feat_ref, top_ref, state_ref,
    gq_ref, gk_ref, gv_ref, gkfeat_ref, gfq_ref, *, size, k
):
    kv_heads = kfeat_ref.shape[1] // (2 * size)
    group = fq_ref.shape[0] // kv_heads
    length = kfeat_ref.shape[0]
    step = STEP
    hidden = jnp.where(place_ref[0] == 0, WIN, 0)
    in_window, col = window_mask(step)
    gk_ref[...] = jnp.zeros_like(gk_ref)
    gv_ref[...] = jnp.zeros_like(gv_ref)
    gkfeat_ref[...] = jnp.zeros_like(gkfeat_ref)
    keys = kv_ref[:, k * size : (k + 1) * size]
    values = with_ones(kv_ref[:, (kv_heads + k) * size : (kv_heads + k + 1) * size], 2)
    kfeat = kfeat_ref[:, k * 2 * size : (k + 1) * 2 * size]
    state = state_ref[k]
    column = lax.broadcasted_iota(jnp.int32, state.shape, 1)
    norm = state[:, size : size + 1]
    state = jnp.where((column == size) | (column == size + 1), norm, state).astype(bf16)
    for g in range(group):
        h = k * group + g
        matrix = fq_ref[h].astype(bf16)
        query = q_ref[:, h * size : (h + 1) * size]
        scaled = (query.astype(f32) * size ** (-0.5)).astype(bf16)
        cols = slice(g * 2 * size, (g + 1) * 2 * size)
        gfq = None
        for at in range(0, length, step):
            end = at + step
            feat = feat_ref[at:end, cols]
            top = top_ref[at:end, cols]
            mask = in_window & (col >= hidden) if at == 0 else in_window
            near = keys[at : end + WIN]
            weight = jnp.where(mask, jnp.exp(dot_nt(scaled[at:end], near)), 0.0)
            grad = (dot_nt(top, values[at : end + WIN]) * weight).astype(bf16)
            gq = dot(grad, near) * size ** (-0.5)
            gk_ref[at : end + WIN] += dot_tn(grad, scaled[at:end])
            gv_ref[at : end + WIN] += dot_tn(weight.astype(bf16), top)
            early = early_mask(step, end)
            linear = jnp.where(early, dot_nt(feat, kfeat[:end]), 0.0).astype(bf16)
            grad = jnp.where(early, dot_nt(top, values[:end]), 0.0).astype(bf16)
            gfeat = dot(grad, kfeat[:end]) + dot_nt(top, state)
            gkfeat_ref[:end] += dot_tn(grad, feat)
            gv_ref[:end] += dot_tn(linear, top)
            mix = softmax_pair_back(feat, gfeat)
            gq_ref[at:end, g * size : (g + 1) * size] = (gq + dot_nt(mix, matrix)).astype(bf16)
            term = dot_tn(query[at:end], mix)
            gfq = term if gfq is None else gfq + term
        gfq_ref[g] = gfq


def key_back(kv_ref, fk_ref, kfeat_ref, later_ref, *refs, size):
    heads = fk_ref.shape[0]
    gks, gvs, gkfeats = refs[:heads], refs[heads : 2 * heads], refs[2 * heads : 3 * heads]
    gkv_ref, halo_ref, gfk_ref = refs[3 * heads :]
    length = kfeat_ref.shape[0]
    for k in range(heads):
        keys = kv_ref[:length, k * size : (k + 1) * size]
        values = with_ones(kv_ref[:length, (heads + k) * size : (heads + k + 1) * size], 2)
        cols = slice(k * 2 * size, (k + 1) * 2 * size)
        later = later_ref[k]
        column = lax.broadcasted_iota(jnp.int32, later.shape, 1)
        norm = later[:, size : size + 1] + later[:, size + 1 : size + 2]
        later = split_column(jnp.where(column == size, norm, later), size)
        kfeat = kfeat_ref[:, cols]
        mix = softmax_pair_back(kfeat, gkfeats[k][...] + dot_nt(values, later))
        gk, gv = slice(k * size, (k + 1) * size), slice((heads + k) * size, (heads + k + 1) * size)
        gkv_ref[:, gk] = gks[k][...]
        gkv_ref[:length, gk] += dot_nt(mix, fk_ref[k].astype(bf16))
        gkv_ref[:, gv] = gvs[k][:, :size]
        gkv_ref[:length, gv] += dot(kfeat, later)[:, :size]
        gfk_ref[k] = dot_tn(keys, mix)
    halo_ref[...] = gkv_ref[:WIN].astype(bf16)


def project_back(
    lane_ref, *refs, kv_heads
):
    gqs = refs[:kv_heads]
    gkv_ref, back_ref, ups_ref, full_ref, tokens_ref, normed_ref, lora_ref = refs[kv_heads : kv_heads + 7]
    gqkv_ref, keep_ref, send_ref, gain_ref, down_ref, up_ref, ext_ref = refs[kv_heads + 7 :]
    length = tokens_ref.shape[0]
    each = gqs[0].shape[1]
    q_cols = each * kv_heads
    all_cols = ups_ref.shape[1]
    for k in range(kv_heads):
        ext_ref[:, k * each : (k + 1) * each] = gqs[k][...]
    ext_ref[: length - WIN, q_cols:all_cols] = gkv_ref[WIN:length].astype(bf16)
    ext_ref[length - WIN :, q_cols:all_cols] = (gkv_ref[length:] + back_ref[...].astype(f32)).astype(bf16)
    gqkv_ref[...] = ext_ref[:, :all_cols]
    ext_ref[:, all_cols:] = dot_nt(ext_ref[:, :all_cols], ups_ref[...].astype(bf16)).astype(bf16)
    down_ref[...] = dot_tn(ext_ref[:, all_cols:], normed_ref[...])[: down_ref.shape[0]]
    up_ref[...] = dot_tn(lora_ref[...], ext_ref[:, :all_cols])[: up_ref.shape[0]]
    chunk = keep_ref.shape[0] // 2
    width = keep_ref.shape[1]
    gain_ref[...] = jnp.zeros_like(gain_ref)
    for ref, masks in ((send_ref, (1, 3)), (keep_ref, (0, 2))):
        for i, m in enumerate(masks):
            at = pl.ds(pl.multiple_of(jnp.bitwise_xor(lane_ref[0], m) * chunk, chunk), chunk)
            rows = tokens_ref[at].astype(f32)
            scale = inverse_rms(rows)
            grad = dot_nt(ext_ref[at], full_ref[...])
            ref[i * chunk : (i + 1) * chunk] = grad.astype(bf16)
            gain_ref[...] += jnp.broadcast_to(
                jnp.sum(grad * rows * scale, 0, keepdims=True), gain_ref.shape
            )


def norm_back(near_ref, got_ref, tokens_ref, vec_ref, middle_ref, out_ref):
    grad = near_ref[...].astype(f32) + got_ref[...].astype(f32)
    values = tokens_ref[...].astype(f32)
    scale = inverse_rms(values)
    scaled = grad * vec_ref[0:1]
    mean = jnp.mean(scaled * values, -1, keepdims=True)
    total = middle_ref[...] + scale * scaled - values * (scale * scale * scale * mean)
    out_ref[...] = total.astype(bf16)


def units_kernel(*refs):
    gu_ref, down_ref, keep_ref, send_ref, hkeep_ref, hsend_ref, ggu_ref = refs[8:]
    half = keep_ref.shape[0]
    units = down_ref.shape[0]
    width = down_ref.shape[1]
    step = 256
    normed = jnp.concatenate([r[...] for r in refs[:4]], 0)
    grad_out = jnp.concatenate([r[...] for r in refs[4:8]], 0)
    for at in range(0, units, step):
        one = slice(at, at + step)
        two = slice(units + at, units + at + step)
        gate = dot(normed, gu_ref[:, one])
        up = dot(normed, gu_ref[:, two])
        grad = dot_nt(grad_out, down_ref[one])
        sigma = 1.0 / (1.0 + jnp.exp(-gate))
        active = gate * sigma
        hidden = (active * up).astype(bf16)
        hkeep_ref[:, one] = hidden[:half]
        hsend_ref[:, one] = hidden[half:]
        ggu_ref[:, one] = (grad * up * sigma * (1.0 + gate * (1.0 - sigma))).astype(bf16)
        ggu_ref[:, two] = (grad * active).astype(bf16)
    for at in range(0, width, 512):
        cols = slice(at, at + 512)
        grad = dot_nt(ggu_ref[...], gu_ref[cols]).astype(bf16)
        keep_ref[:, cols] = grad[:half]
        send_ref[:, cols] = grad[half:]


def blocks_of_product(place_ref, *refs, lefts, rights, groups, picks):
    left, right = refs[:lefts], refs[lefts : lefts + rights]
    out = refs[-1]
    rows = out.shape[0] // len(picks)

    def joined(pieces):
        return jnp.concatenate(pieces, 0) if len(pieces) > 1 else pieces[0]

    for i, pick in enumerate(picks):
        at = pl.multiple_of(jnp.bitwise_xor(place_ref[0], pick) * rows, rows)
        total = None
        for d in range(groups):
            own = slice(d * lefts // groups, (d + 1) * lefts // groups)
            part = joined([r[:, pl.ds(at, rows)] for r in left[own]])
            own = slice(d * rights // groups, (d + 1) * rights // groups)
            term = dot_tn(part, joined([r[...] for r in right[own]]))
            total = term if total is None else total + term
        out[i * rows : (i + 1) * rows] = total.astype(bf16)


def out_blocks(place_ref, left_ref, right_ref, keep_ref, send_ref, sum_ref, *, pair):
    sum_ref[...] = dot_tn(left_ref[...], right_ref[...])
    count = RING * pair
    rows = sum_ref.shape[0] // count
    for i in range(count):
        at = pl.multiple_of(jnp.bitwise_xor(place_ref[0], i) * rows, rows)
        d, beta = i // pair, i % pair
        part = sum_ref[pl.ds(at, rows)].astype(bf16)
        d = (0, 2, 1, 3)[d]
        if beta == 0:
            keep_ref[d * rows : (d + 1) * rows] = part
        else:
            to = (beta - 1) * RING + d
            send_ref[to * rows : (to + 1) * rows] = part


def pack_small(place_ref, gfk_ref, up_ref, down_ref, outu_ref, two_ref, one_ref, *refs, kv_heads, group):
    gfqs, out_ref = refs[:kv_heads], refs[-1]
    count = out_ref.shape[0]
    size = gfk_ref.shape[2]
    each = size // count
    rank = up_ref.shape[0] // 3
    q_cols = kv_heads * group * size
    kv_cols = kv_heads * size
    q_each, kv_each = q_cols // count, kv_cols // count
    vec_cols = down_ref.shape[1] // count
    vec_rows = 48

    def wide(value, rows):
        if value.shape[1] < LANES:
            value = jnp.concatenate([value, jnp.zeros((value.shape[0], LANES - value.shape[1]), f32)], 1)
        if value.shape[0] < rows:
            value = jnp.concatenate([value, jnp.zeros((rows - value.shape[0], LANES), f32)], 0)
        return value

    for s in range(count):
        own = slice(s * each, (s + 1) * each)
        fq = jnp.concatenate([gfqs[k][g, own] for k in range(kv_heads) for g in range(group)], 0)
        fk = jnp.concatenate([gfk_ref[k, own] for k in range(kv_heads)], 0)
        kv = [
            up_ref[(c + 1) * rank : (c + 2) * rank, q_cols + c * kv_cols + s * kv_each : q_cols + c * kv_cols + (s + 1) * kv_each]
            for c in range(2)
        ]
        q = up_ref[:rank, s * q_each : (s + 1) * q_each]
        groups = [wide(fq, fq.shape[0]), wide(fk, 16), wide(jnp.concatenate(kv, 0), 16), wide(q, 16)]
        for at in range(s * vec_cols, (s + 1) * vec_cols, min(LANES, vec_cols)):
            cols = slice(at, at + min(LANES, vec_cols))
            vec = [down_ref[:, cols], outu_ref[:, cols], two_ref[:1, cols], one_ref[:1, cols]]
            groups.append(wide(jnp.concatenate(vec, 0), vec_rows))
        away = jnp.bitwise_xor(place_ref[0], s)
        to, bit = 0, 1
        while bit < count:
            to = to + jnp.where((away & bit) != 0, count // (2 * bit), 0)
            bit *= 2
        out_ref[pl.ds(to, 1)] = jnp.concatenate(groups, 0).astype(bf16)[None]


def per_device(
    tokens,
    attention_norm_gain,
    query_weight,
    key_value_weight,
    output_weight,
    adapter_down_matrices,
    adapter_query_up,
    adapter_key_value_up,
    adapter_output_down,
    adapter_output_up,
    query_feature_matrix,
    key_feature_matrix,
    feedforward_norm_gain,
    gate_weight,
    up_weight,
    down_weight,
    cotangent,
):
    count = lax.axis_size(SEQ)
    pair = count // RING
    place = lax.axis_index(SEQ)
    along, beside = place // pair, place % pair
    lane = lax.axis_index("kv")
    unused, length, width = tokens.shape
    depth, q_cols = query_weight.shape
    kv_cols = key_value_weight.shape[2]
    heads, head_size = query_feature_matrix.shape[0], query_feature_matrix.shape[2]
    kv_heads = key_feature_matrix.shape[0]
    group = heads // kv_heads
    rank = adapter_query_up.shape[0]
    all_cols = q_cols + 2 * kv_cols
    wide_size = 2 * head_size
    chunk = length // lax.axis_size("kv")
    rows_out = output_weight.shape[0]
    units_each = down_weight.shape[0]
    units = gate_weight.shape[1] // RING
    here = place.astype(jnp.int32)[None]
    lane_here = lane.astype(jnp.int32)[None]
    order = [place ^ i for i in range(count)]
    nears = [lane ^ k for k in (0, 2, 1, 3)]
    rings = [d * pair for d in range(RING)]
    x = tokens[0]
    dy = cotangent[0]

    def across(array, *gates):
        result = [array]
        bit = 1
        while bit < pair:
            result = result + [trade(after(a, *gates), SEQ, bit) for a in result]
            bit *= 2
        return result

    def across_sum(parts, *gates):
        bit = pair // 2
        while bit:
            parts = [
                add_low(parts[i], after(trade(parts[i + bit], SEQ, bit), *gates)) for i in range(bit)
            ]
            bit //= 2
        return parts[0]

    parameters = [
        jnp.swapaxes(adapter_down_matrices, 1, 2),
        query_feature_matrix.reshape(-1, head_size),
        adapter_output_down.T,
        key_feature_matrix.reshape(-1, head_size),
        adapter_key_value_up.reshape(2 * rank, -1),
        adapter_query_up,
        jnp.stack([attention_norm_gain, feedforward_norm_gain]),
        adapter_output_up,
    ]
    packed = pl.pallas_call(
        pack_weights,
        out_shape=shape((depth, all_cols + LANES), bf16),
        in_specs=[pl.BlockSpec(memory_space=pltpu.HBM)] * (2 + len(parameters)),
        out_specs=pl.BlockSpec(memory_space=pltpu.VMEM),
        scratch_shapes=[pltpu.VMEM(p.shape, bf16) for p in parameters]
        + [pltpu.SemaphoreType.DMA((3 + len(parameters),))],
        compiler_params=pltpu.CompilerParams(vmem_limit_bytes=12 * 2**20),
    )(query_weight, key_value_weight, *parameters)
    got = [packed, trade(packed, SEQ, rings[1]), trade(packed, SEQ, rings[2])]
    halo = moved(x[length - WIN :], SEQ, 1)
    pieces = [across(packed)]

    cuts = own_call(
        cut_units,
        [shape((depth, 2 * units), bf16)] * RING,
        [jnp.stack([along ^ d for d in range(RING)]).astype(jnp.int32), gate_weight, up_weight],
        1,
    )
    own_gu = across(cuts[0], got[2], pieces[0][-1], halo)
    pieces.append(across(got[1]))
    pieces.append(across(got[2]))
    got.append(trade(got[2], SEQ, rings[1]))
    pieces.append(across(got[3]))
    last_piece = pieces[3][-1]
    out_got = [output_weight] + [trade(after(output_weight, pieces[1][-1], pieces[0][-1], halo), SEQ, m) for m in rings[1:3]]
    gu_got = [cuts[0], None, None, None]
    gu_got[2] = trade(after(cuts[2], *out_got[1:]), SEQ, rings[2])
    out_got.append(trade(out_got[2], SEQ, rings[1]))
    gu_got[1] = trade(after(cuts[1], out_got[3]), SEQ, rings[1])
    out_first = across(jnp.concatenate(out_got[:2], 0), last_piece)

    own_x = block(x, lane, chunk)
    own_dy = block(dy, lane, chunk)
    dy_blocks = [[block(dy, k, chunk) for k in nears]]
    full, fq_w, fk_w, ups, out_down, vecs = placed(
        [pieces[d][b] for d in range(RING) for b in range(pair)],
        depth,
        order,
        functools.partial(unpack_weights, count=count),
        [
            shape((heads, head_size, head_size), f32),
            shape((kv_heads, head_size, head_size), f32),
            shape((LANES, all_cols), f32),
            shape((q_cols, LANES), f32),
            shape((8 + rank, width), f32),
        ],
        deps=[own_x, own_gu[-1]] + dy_blocks[0],
    )

    normed, lora, query, kv_ext, key_feat, totals = own_call(
        functools.partial(project, size=head_size),
        [
            shape((length, width), bf16),
            shape((length, LANES), bf16),
            shape((length, q_cols), bf16),
            shape((length + WIN, 2 * kv_cols), bf16),
            shape((length, kv_heads * wide_size), bf16),
            shape((kv_heads, wide_size, wide_size), f32),
        ],
        [here, halo, x, full, vecs, ups, fk_w],
        1,
    )
    def running(total, sign, between, beside=True):
        result = jnp.zeros_like(total)
        results, steps = [], []
        bit = 1
        while bit < count:
            other = trade(total, SEQ, bit)
            if len(results) < len(between):
                results.append(between[len(results)](*(steps[-1:] if beside else [other])))
                if beside:
                    other = after(other, results[-1][0])
            steps.append(other)
            mine = (place & bit) != 0 if sign > 0 else (place & bit) == 0
            result = result + jnp.where(mine, other, 0.0)
            total = total + other
            bit *= 2
        return result, results, steps

    states, unused, steps = running(totals, 1, [])
    local = own_call(
        functools.partial(local_attention, size=head_size),
        [shape((length, group * wide_size), f32)] * kv_heads
        + [shape((length, group * wide_size), bf16)] * kv_heads,
        [here, query, kv_ext, fq_w, key_feat],
        1,
        deps=[steps[1], gu_got[1], gu_got[2]],
    )
    accs, feats = list(local[:kv_heads]), list(local[kv_heads:])
    out_second = across(jnp.concatenate(out_got[2:], 0), steps[0])
    gu_got[3] = trade(after(cuts[3], states), SEQ, rings[3])
    dy_got = [None, trade(after(own_dy, states), SEQ, rings[1])]
    out_w = placed(
        out_first + out_second,
        rows_out,
        [order[rings[d] + b] for b in range(pair) for d in (0, 1)]
        + [order[rings[d] + b] for b in range(pair) for d in (2, 3)],
    )
    gu_mid = across(jnp.concatenate([gu_got[1], gu_got[2]], 0))
    tops, attended, keep, send = own_call(
        functools.partial(finish_attention, size=head_size, kv_heads=kv_heads),
        [
            shape((length, heads * wide_size), f32),
            shape((length, q_cols), bf16),
            shape((2 * chunk, width + LANES), bf16),
            shape((2 * chunk, width + LANES), bf16),
        ],
        [lane_here] + accs + feats + [states, out_w, out_down],
        1,
        deps=[],
    )
    downs = across(down_weight, gu_mid[-1])

    def kv_sums(keep, send, *gates):
        other = after(trade(send, "kv", 1), *gates)
        near = add_low(keep[:chunk], other[:chunk])
        side = add_low(keep[chunk:], other[chunk:])
        return near, trade(side, "kv", 2)

    def kv_all(own, *gates):
        side = trade(own, "kv", 2)
        return own, side, trade(own, "kv", 1), trade(after(side, *gates), "kv", 1)

    near, other = kv_sums(keep, send)
    middle, normed_two, lora_out = own_call(
        residual_norm,
        [shape((chunk, width), f32), shape((chunk, width), bf16), shape((chunk, LANES), bf16)],
        [near, other, own_x, vecs],
        deps=[gu_got[3]],
    )

    n_got = [normed_two, None, None, None]
    n_got[2] = trade(normed_two, SEQ, rings[2])
    n_got[1] = trade(normed_two, SEQ, rings[1])
    gu_last = across(gu_got[3])
    n_first = kv_all(normed_two, gu_mid[-1], downs[-1], gu_last[-1])
    n_got[3] = trade(n_got[2], SEQ, rings[1])
    dy_got.append(trade(after(own_dy, n_got[1]), SEQ, rings[2]))
    dy_got.append(trade(after(dy_got[2], n_got[3]), SEQ, rings[1]))
    dy_blocks.append(kv_all(after(dy_got[1], normed_two)))
    gu_w = placed(
        [after(g, normed_two) for g in own_gu + gu_mid + gu_last],
        depth,
        [order[b] for b in range(pair)]
        + [order[rings[d] + b] for b in range(pair) for d in (1, 2)]
        + [order[rings[3] + b] for b in range(pair)],
    )
    down_w = placed([after(w, normed_two) for w in downs], units_each, [beside ^ b for b in range(pair)])
    n_blocks = []
    keeps, hiddens, ggus = [], [], []
    sums = [None] * RING
    halves = [None] * RING
    for d in range(RING):
        n_blocks.append(n_first if d == 0 else kv_all(n_got[d]))
        if d == 0:
            ready = []
        elif d == 1:
            ready = [n_got[3], dy_got[2], kv_all(n_got[2])[1]]
        else:
            ready = [halves[d - 2][0], halves[d - 2][1]]
        if d == 2:
            ready.append(kv_all(n_got[3])[1])
        if d > 1:
            dy_blocks.append(kv_all(dy_got[d]))
        keep, send, hkeep, hsend, ggu = own_call(
            units_kernel,
            [shape((2 * chunk, width), bf16)] * 2
            + [shape((2 * chunk, units), bf16)] * 2
            + [shape((4 * chunk, 2 * units), bf16)],
            list(n_blocks[d]) + list(dy_blocks[d]) + [gu_w, down_w],
            deps=ready + keeps[-1:],
        )
        keeps.append(keep)
        other = trade(send, "kv", 1)
        halves[d] = (add_low(keep[:chunk], other[:chunk]), add_low(keep[chunk:], other[chunk:]))
        hiddens.append((hkeep, hsend))
        ggus.append(ggu)
    def product(left, right, picks, rows, groups=RING, at=here, deps=()):
        if rows % LANES == 0:
            return own_call(
                functools.partial(
                    blocks_of_product, lefts=len(left), rights=len(right), groups=groups, picks=picks
                ),
                [shape((rows * len(picks), right[0].shape[1]), bf16)],
                [at] + left + right,
                1,
                deps=deps,
            )[0]
        result = dot_tn(jnp.concatenate(left, 0), jnp.concatenate(right, 0)).astype(bf16)
        return jnp.concatenate([block(result, at[0] ^ i, rows) for i in picks], 0)

    n_all = [p for n in n_blocks for p in n]
    picks = [[m + b for m in rings] for b in range(pair)]
    gu_parts = [None] * pair
    for b in range(1, pair):
        gu_parts[b] = [product(n_all, ggus, p, depth, deps=halves[3]) for p in (picks[b][2:], picks[b][:2])]
    firsts = [p for part in gu_parts[1:] for p in part]
    sums = [None] * RING
    for d in (0, 3, 2, 1):
        side = halves[d][1]
        sums[d] = add_low(after(halves[d][0], *firsts) if d == 3 else halves[d][0], trade(side, "kv", 2))
    rest = [trade(sums[d], SEQ, rings[d]) for d in (1, 2, 3)]
    gu_parts[0] = [product(n_all, ggus, p, depth, deps=[sums[3]]) for p in (picks[0][2:], picks[0][:2])]
    far_cols = across_sum([p[0] for p in gu_parts])
    hidden_all = [p for h in hiddens for p in h]
    dy_all = [p for b in dy_blocks for p in b]
    beside_here = beside.astype(jnp.int32)[None]
    down_parts = [None] * pair
    for b in reversed(range(pair)):
        down_parts[b] = product(
            hidden_all, dy_all, [b], units_each, RING, beside_here, [sums[3]]
        )
    grad_middle, grad_branch, gain_two, out_up_part = own_call(
        residual_norm_back,
        [
            shape((chunk, width), f32),
            shape((chunk, width), bf16),
            shape((8, width), f32),
            shape((rank, width), f32),
        ],
        [sums[0]] + rest + [middle, vecs, own_dy, lora_out],
        deps=gu_parts[0] + down_parts + [far_cols],
    )

    all_branch = kv_all(grad_branch)

    hkeep = jnp.concatenate([h[0] for h in hiddens], 0)
    hsend = jnp.concatenate([h[1] for h in hiddens], 0)
    down_send = dot(after(hsend, grad_branch), down_w).astype(bf16)
    down_keep = dot(after(hkeep, grad_branch), down_w).astype(bf16)
    near_cols = across_sum([p[1] for p in gu_parts])
    down_other = trade(down_send, "kv", 1)
    gate_parts = [near_cols[:depth], None, None, None]
    gate_parts[2] = trade(far_cols[:depth], SEQ, rings[2])
    gate_parts[3] = trade(after(far_cols[depth:], all_branch[1]), SEQ, rings[3])
    results = own_call(
        functools.partial(attended_back, size=head_size, kv_heads=kv_heads),
        [shape((length, group * wide_size), bf16)] * kv_heads
        + [shape((kv_heads, wide_size, wide_size), f32), shape((length, width + LANES), bf16)],
        [lane_here] + list(all_branch) + [out_w, out_down, vecs, tops] + feats,
        1,
        [pltpu.VMEM((length, q_cols), f32)],
        deps=[],
    )
    grad_tops, grad_state, branch_rows = results[:kv_heads], results[kv_heads], results[kv_heads + 1]
    other = down_other.reshape(RING, 2, chunk, width)
    down_keep = down_keep.reshape(RING, 2, chunk, width)
    near = add_low(down_keep[:, 0], other[:, 0])
    side = add_low(down_keep[:, 1], other[:, 1])
    high = trade(after(side[2:], all_branch[1]), "kv", 2)
    down_sum = across_sum(down_parts)
    out_keep, out_send = own_call(
        functools.partial(out_blocks, pair=pair),
        [
            shape((RING * rows_out, width + LANES), bf16),
            shape(((pair - 1) * RING * rows_out, width + LANES), bf16),
        ],
        [here, attended, branch_rows],
        1,
        [pltpu.VMEM((q_cols, width + LANES), f32)],
    )
    out_parts = [out_keep] + [
        out_send[b * RING * rows_out : (b + 1) * RING * rows_out] for b in range(pair - 1)
    ]

    def attend_back(k, *step):
        return own_call(
            functools.partial(local_back, size=head_size, k=k),
            [
                shape((length, group * head_size), bf16),
                shape((length + WIN, head_size), f32),
                shape((length + WIN, wide_size), f32),
                shape((length, wide_size), f32),
                shape((group, head_size, head_size), f32),
            ],
            [here, query, kv_ext, fq_w, key_feat, feats[k], grad_tops[k], states],
            1,
            deps=list(step) + ([high, gate_parts[3]] if k else [side, out_send, down_sum, gate_parts[2]]),
        )

    later, local, steps = running(grad_state, -1, [functools.partial(attend_back, k) for k in range(kv_heads)])
    gate_parts[1] = trade(near_cols[depth:], SEQ, rings[1])
    low = trade(after(side[:2], high), "kv", 2)
    high = add_low(near[2:], high)
    low = add_low(near[:2], low)
    out_sum = across_sum([out_keep] + [after(p, steps[0]) for p in out_parts[1:]], local[0][0])
    mixed = trade(jnp.concatenate([high[1], low[1]], 0), SEQ, rings[1])
    out_half = 2 * rows_out
    out_other = trade(out_sum[out_half:], SEQ, rings[1])
    grad_kv, halo_back, grad_fk = own_call(
        functools.partial(key_back, size=head_size),
        [
            shape((length + WIN, 2 * kv_cols), f32),
            shape((WIN, 2 * kv_cols), bf16),
            shape((kv_heads, head_size, head_size), f32),
        ],
        [kv_ext, fk_w, key_feat, later] + [l[1] for l in local] + [l[2] for l in local] + [l[3] for l in local],
    )
    returned = moved(halo_back, SEQ, -1)

    gqkv, grad_keep, grad_send, gain_one, lora_down, up_all, ext = own_call(
        functools.partial(project_back, kv_heads=kv_heads),
        [
            shape((length, all_cols), bf16),
            shape((2 * chunk, width), bf16),
            shape((2 * chunk, width), bf16),
            shape((8, width), f32),
            shape((3 * rank, width), f32),
            shape((3 * rank, all_cols), f32),
            shape((length, all_cols + LANES), bf16),
        ],
        [lane_here] + [l[0] for l in local] + [grad_kv, returned, ups, full, x, normed, lora],
        1,
    )
    near, other = kv_sums(grad_keep, grad_send)
    qkv_parts = [None] * pair
    for b in reversed(range(pair)):
        qkv_parts[b] = [product([normed], [gqkv], p, depth, 1, deps=[near]) for p in (picks[b][2:], picks[b][:2])]

    qkv_high = across_sum([p[0] for p in qkv_parts])
    qkv_low = across_sum([p[1] for p in qkv_parts])
    (own_grad,) = own_call(
        norm_back, [shape((chunk, width), bf16)], [near, other, own_x, vecs, grad_middle],
        deps=[qkv_high],
    )
    all_grad = kv_all(own_grad)

    vec_cols = width // count
    fq_rows = heads * head_size // count
    fk_rows = kv_heads * head_size // count
    small_rows = fq_rows + 48 + 48 * max(1, vec_cols // LANES)
    (small,) = own_call(
        functools.partial(pack_small, kv_heads=kv_heads, group=group),
        [shape((count, small_rows, LANES), bf16)],
        [here, grad_fk, up_all, lora_down, out_up_part, gain_two, gain_one] + [l[4] for l in local],
        1,
        deps=[own_grad],
    )
    half, bit = count // 2, 1
    while half:
        small = add_low(small[:half], trade(small[half:], SEQ, bit))
        half, bit = half // 2, 2 * bit
    qkv_far = add_low(qkv_high[:depth], trade(qkv_high[depth:], SEQ, rings[1]))
    qkv_near = add_low(qkv_low[:depth], trade(qkv_low[depth:], SEQ, rings[1]))
    grad_w = qkv_near.astype(f32) + trade(qkv_far, SEQ, rings[2]).astype(f32)
    grad_w_query = grad_w[:, :q_cols]
    grad_w_kv = jnp.stack([grad_w[:, q_cols : q_cols + kv_cols], grad_w[:, q_cols + kv_cols :]])

    (grad_tokens,) = own_call(
        rows_placed, [shape((length, width), f32)], [jnp.stack(nears).astype(jnp.int32), *all_grad], 1
    )

    mixed = after(mixed, own_grad)
    high = add_low(high[0], mixed[:chunk])
    low = add_low(low[0], mixed[chunk:])
    ffn_out = add_low(low, trade(high, SEQ, rings[2])).astype(f32)
    own_out = (middle + ffn_out).astype(bf16)
    all_out = kv_all(own_out)
    (output,) = own_call(
        rows_placed, [shape((length, width), bf16)], [jnp.stack(nears).astype(jnp.int32), *all_out], 1
    )
    out_sum = add_low(after(out_sum[:out_half], own_grad), out_other)
    out_sum = add_low(out_sum[:rows_out], trade(out_sum[rows_out:], SEQ, rings[2])).astype(f32)
    grad_w_gate, grad_w_up = own_call(
        place_units,
        [shape(gate_weight.shape, f32)] * 2,
        [jnp.stack([along ^ d for d in range(RING)]).astype(jnp.int32)]
        + gate_parts,
        1,
        deps=[own_grad],
    )

    small = small[0]
    at = fq_rows
    grad_fmap_query = small[:at, :head_size].astype(f32).reshape(query_feature_matrix.shape)
    grad_fmap_key = small[at : at + fk_rows, :head_size].astype(f32).reshape(key_feature_matrix.shape)
    at += 16
    kv_each, q_each = kv_cols // count, q_cols // count
    grad_lora_up_kv = small[at : at + 2 * rank, :kv_each].astype(f32).reshape(2, rank, kv_each)
    at += 16
    grad_lora_up_query = small[at : at + rank, :q_each].astype(f32)
    at += 16
    total = small[at:]
    for mask in (1, 2):
        total = lax.optimization_barrier(total)
        total = add_low(total, trade(total, "kv", mask))
    total = lax.optimization_barrier(total).astype(f32)
    each = min(LANES, vec_cols)
    total = jnp.concatenate(
        [total[i * 48 : (i + 1) * 48, :each] for i in range(vec_cols // each)], 1
    )
    grad_lora_down = jnp.transpose(total[: 3 * rank].reshape(3, rank, depth), (0, 2, 1))
    grad_lora_up_out = total[3 * rank : 4 * rank]
    grad_g_mlp = total[4 * rank]
    grad_g_attn = total[4 * rank + 1]
    return (
        output[None],
        grad_tokens[None],
        grad_g_attn,
        grad_w_query,
        grad_w_kv,
        out_sum[:, :width],
        grad_lora_down,
        grad_lora_up_query,
        grad_lora_up_kv,
        out_sum[:, width : width + rank],
        grad_lora_up_out,
        grad_fmap_query,
        grad_fmap_key,
        grad_g_mlp,
        grad_w_gate,
        grad_w_up,
        down_sum.astype(f32),
    )


def solution(mesh):
    devices = mesh.devices
    count, kv = devices.shape
    mesh = Mesh(devices.reshape(RING, count // RING, kv), SEQ + ("kv",))
    return jax.shard_map(
        per_device,
        mesh=mesh,
        in_specs=(
            P(None, SEQ, None),
            P(SEQ),
            P(SEQ, "kv"),
            P(None, SEQ, "kv"),
            P(("kv",) + SEQ, None),
            P(None, SEQ, None),
            P(None, ("kv",) + SEQ),
            P(None, None, ("kv",) + SEQ),
            P(("kv",) + SEQ, None),
            P(None, SEQ),
            P("kv", SEQ, None),
            P("kv", SEQ, None),
            P(SEQ),
            P(SEQ, "kv"),
            P(SEQ, "kv"),
            P(("kv",) + SEQ, None),
            P(None, SEQ, None),
        ),
        out_specs=(
            P(None, SEQ, None),
            P(None, SEQ, None),
            P(SEQ),
            P(SEQ, "kv"),
            P(None, SEQ, "kv"),
            P(("kv",) + SEQ, None),
            P(None, SEQ, None),
            P(None, ("kv",) + SEQ),
            P(None, None, ("kv",) + SEQ),
            P(("kv",) + SEQ, None),
            P(None, SEQ),
            P("kv", SEQ, None),
            P("kv", SEQ, None),
            P(SEQ),
            P(SEQ, "kv"),
            P(SEQ, "kv"),
            P(("kv",) + SEQ, None),
        ),
        check_vma=False,
    )
```

```python
import functools

import jax
import jax.numpy as jnp
from jax import lax
from jax.experimental import pallas as pl
from jax.experimental.pallas import tpu as pltpu
from jax.sharding import Mesh, PartitionSpec as P

WIN = 64
RING = 4
SEQ = ("ring", "pair")
STEP = 128
SMALL = 80
LANES = 128
epsilon = 1e-05
bf16 = jnp.bfloat16
f32 = jnp.float32
shape = jax.ShapeDtypeStruct


def trade(array, axis, mask):
    count = lax.axis_size(axis)
    return lax.ppermute(array, axis, [(i, i ^ mask) for i in range(count)])


def moved(array, axis, by):
    count = lax.axis_size(axis)
    pairs = [(i, i + by) for i in range(count) if 0 <= i + by < count]
    return lax.ppermute(array, axis, pairs)


def after(value, *earlier):
    return lax.optimization_barrier((value,) + earlier)[0]


def dot(a, b):
    return jnp.dot(a, b, preferred_element_type=f32)


def dot_nt(a, b):
    return lax.dot_general(a, b, (((1,), (1,)), ((), ())), preferred_element_type=f32)


def dot_tn(a, b):
    return lax.dot_general(a, b, (((0,), (0,)), ((), ())), preferred_element_type=f32)


def add_low(a, b):
    return (a.astype(f32) + b.astype(f32)).astype(bf16)


def block(array, at, rows, axis=0):
    return lax.dynamic_slice_in_dim(array, at * rows, rows, axis)


def own_call(body, outs, inputs, scalars=0, scratch=(), flops=0, room=8, deps=(), hbm=0):
    count, deps = len(inputs), list(deps)

    def run(*refs):
        body(*refs[:count], *refs[count + len(deps) :])

    vmem = pl.BlockSpec(memory_space=pltpu.VMEM)
    smem = pl.BlockSpec(memory_space=pltpu.SMEM)
    size = sum(a.size * a.dtype.itemsize for a in list(inputs)[: count - hbm] + list(outs))
    return pl.pallas_call(
        run,
        out_shape=tuple(outs),
        in_specs=[smem] * scalars
        + [vmem] * (count - scalars - hbm)
        + [pl.BlockSpec(memory_space=pl.ANY)] * (hbm + len(deps)),
        out_specs=tuple(vmem for _ in outs),
        scratch_shapes=list(scratch),
        compiler_params=pltpu.CompilerParams(vmem_limit_bytes=size + room * 2**20),
        cost_estimate=pl.CostEstimate(flops=flops, bytes_accessed=0, transcendentals=0),
    )(*inputs, *deps)


def placed(pieces, rows, order, extra=None, outs=(), more=(), deps=()):
    count = len(pieces)

    def body(order_ref, *refs):
        refs = refs[: count + len(more)] + refs[count + len(more) + len(deps) :]
        out, sems = refs[count + len(more)], refs[-1]
        copies = []
        i = 0
        for piece in refs[:count]:
            for inner in range(0, piece.shape[0], rows):
                at = pl.multiple_of(order_ref[i] * rows, rows)
                copies.append(
                    pltpu.make_async_copy(piece.at[pl.ds(inner, rows)], out.at[pl.ds(at, rows)], sems.at[i])
                )
                copies[-1].start()
                i += 1
        for copy in copies:
            copy.wait()
        if extra is not None:
            extra(out, *refs[count : count + len(more)], *refs[count + len(more) + 1 : -1])

    vmem = pl.BlockSpec(memory_space=pltpu.VMEM)
    total = sum(p.shape[0] for p in pieces)
    result = pl.pallas_call(
        body,
        out_shape=(shape((total, pieces[0].shape[1]), pieces[0].dtype),) + tuple(outs),
        in_specs=[pl.BlockSpec(memory_space=pltpu.SMEM)]
        + [pl.BlockSpec(memory_space=pl.ANY)] * count
        + [vmem] * len(more)
        + [pl.BlockSpec(memory_space=pl.ANY)] * len(deps),
        out_specs=(vmem,) * (1 + len(outs)),
        scratch_shapes=[pltpu.SemaphoreType.DMA((total // rows,))],
        compiler_params=pltpu.CompilerParams(vmem_limit_bytes=16 * 2**20),
        cost_estimate=pl.CostEstimate(flops=0, bytes_accessed=0, transcendentals=0),
    )(jnp.stack(order).astype(jnp.int32), *pieces, *more, *deps)
    return result if outs else result[0]


def rows_placed(order_ref, *refs):
    out = refs[-1]
    each = STEP
    at = 0
    for ref in refs[:-1]:
        for inner in range(0, ref.shape[0], each):
            to = pl.multiple_of(order_ref[at] * each, each)
            out[pl.ds(to, each)] = ref[inner : inner + each].astype(out.dtype)
            at += 1


def pack_weights(*refs):
    q_hbm, kv_hbm = refs[:2]
    number = (len(refs) - 4) // 2
    out_ref, held, sems = refs[2 + number], refs[3 + number : -1], refs[-1]
    depth, q_cols = q_hbm.shape
    kv_cols = kv_hbm.shape[2]
    moves = [(q_hbm, out_ref.at[:, :q_cols])]
    for c in range(2):
        moves.append((kv_hbm.at[c], out_ref.at[:, pl.ds(q_cols + c * kv_cols, kv_cols)]))
    moves += list(zip(refs[2 : 2 + number], held))
    copies = [pltpu.make_async_copy(a, b, sems.at[i]) for i, (a, b) in enumerate(moves)]
    for copy in copies:
        copy.start()
    for copy in copies:
        copy.wait()
    down_ref, fq_ref, outd_ref, fk_ref, kvup_ref, qup_ref, gain_ref, outu_ref = held
    lora = down_ref.shape[0] * down_ref.shape[1]
    rank = down_ref.shape[1]
    size = fq_ref.shape[1]

    def wide(value, rows, cols):
        value = value.astype(f32)
        if value.shape[1] < cols:
            value = jnp.concatenate([value, jnp.zeros((value.shape[0], cols - value.shape[1]), f32)], 1)
        if value.shape[0] < rows:
            value = jnp.concatenate([value, jnp.zeros((rows - value.shape[0], cols), f32)], 0)
        return value

    downs = [wide(down_ref[c], rank, depth) for c in range(down_ref.shape[0])]
    gap = jnp.zeros((size, depth), f32)
    outd = wide(outd_ref[...], rank, depth)
    rest = jnp.zeros((LANES - lora - size - rank, depth), f32)
    tall = jnp.concatenate(downs + [gap, outd, rest], 0)
    groups = [
        wide(fq_ref[...], fq_ref.shape[0], SMALL),
        wide(fk_ref[...], 16, SMALL),
        wide(jnp.concatenate([kvup_ref[...].astype(f32), wide(qup_ref[...], 2 * rank, qup_ref.shape[1])], 1), 16, SMALL),
    ]
    vec = jnp.concatenate(
        [gain_ref[...].astype(f32), outu_ref[...].astype(f32)], 0
    )
    for at in range(0, depth, 64):
        groups.append(wide(vec[:, at : at + 64], 16, SMALL))
    small = wide(jnp.concatenate(groups, 0), depth, SMALL)
    small = jnp.concatenate(
        [jnp.zeros((depth, lora), f32), small, jnp.zeros((depth, LANES - lora - SMALL), f32)], 1
    )
    out_ref[:, q_cols + 2 * kv_cols :] = (tall.T + small).astype(bf16)


def unpack_weights(full_ref, fq_ref, fk_ref, ups_ref, outd_ref, vec_ref, *, count):
    depth = full_ref.shape[0] // count
    all_cols = full_ref.shape[1] - LANES
    heads, size = fq_ref.shape[0], fq_ref.shape[2]
    kv_heads = fk_ref.shape[0]
    rank = vec_ref.shape[0] - 8
    each = size // count
    lora = 3 * rank
    q_cols = heads * size
    kv_cols = kv_heads * size
    q_each, kv_each = q_cols // count, kv_cols // count
    fq_rows = heads * each
    ups_ref[...] = jnp.zeros_like(ups_ref)
    outd_ref[...] = jnp.zeros_like(outd_ref)
    vec_ref[...] = jnp.zeros_like(vec_ref)
    for s in range(count):
        part = full_ref[s * depth : (s + 1) * depth, all_cols:].astype(f32)
        small = part[:, lora : lora + SMALL]
        for h in range(heads):
            fq_ref[h, s * each : (s + 1) * each] = small[h * each : (h + 1) * each, :size]
        outd_ref[s * fq_rows : (s + 1) * fq_rows, :rank] = small[:fq_rows, size : size + rank]
        at = fq_rows
        for h in range(kv_heads):
            fk_ref[h, s * each : (s + 1) * each] = small[at + h * each : at + (h + 1) * each, :size]
        at += 16
        ups_ref[:rank, s * q_each : (s + 1) * q_each] = small[at : at + rank, kv_each : kv_each + q_each]
        for c in range(2):
            to = q_cols + c * kv_cols + s * kv_each
            ups_ref[(c + 1) * rank : (c + 2) * rank, to : to + kv_each] = small[
                at + c * rank : at + (c + 1) * rank, :kv_each
            ]
        at += 16
        for q in range(depth // 64):
            to = s * depth + q * 64
            vec_ref[:, to : to + 64] = small[at : at + 16, :64]
            at += 16


def cut_units(at_ref, gate_ref, up_ref, *outs):
    units = outs[0].shape[1] // 2
    for i, out in enumerate(outs):
        at = pl.multiple_of(at_ref[i] * units, units)
        out[:, :units] = gate_ref[:, pl.ds(at, units)]
        out[:, units:] = up_ref[:, pl.ds(at, units)]


def place_units(at_ref, *refs):
    gate_ref, up_ref = refs[-2:]
    units = refs[0].shape[1] // 2
    for i, ref in enumerate(refs[:-2]):
        at = pl.multiple_of(at_ref[i] * units, units)
        gate_ref[:, pl.ds(at, units)] = ref[:, :units].astype(f32)
        up_ref[:, pl.ds(at, units)] = ref[:, units:].astype(f32)


def softmax_pair(mixing):
    up = jnp.exp(mixing - jnp.max(mixing, -1, keepdims=True))
    down = jnp.exp(jnp.min(mixing, -1, keepdims=True) - mixing)
    up = up / jnp.sum(up, -1, keepdims=True)
    down = down / jnp.sum(down, -1, keepdims=True)
    return jnp.concatenate([up, down], -1).astype(bf16)


def softmax_pair_back(feat, grad):
    size = feat.shape[1] // 2
    feat = feat.astype(f32)
    term = feat * grad.astype(bf16).astype(f32)
    is_up = lax.broadcasted_iota(jnp.int32, term.shape, 1) < size
    up_sum = jnp.sum(jnp.where(is_up, term, 0.0), -1, keepdims=True)
    down_sum = jnp.sum(jnp.where(is_up, 0.0, term), -1, keepdims=True)
    term = term - feat * jnp.where(is_up, up_sum, down_sum)
    return (term[:, :size] - term[:, size:]).astype(bf16)


def with_ones(values, ones):
    rows, size = values.shape
    column = lax.broadcasted_iota(jnp.int32, (rows, size), 1)
    return jnp.concatenate([values, jnp.where(column < ones, 1.0, 0.0).astype(values.dtype)], 1)


def split_column(wide, size):
    column = lax.broadcasted_iota(jnp.int32, wide.shape, 1)
    total = wide[:, size : size + 1]
    high = total.astype(bf16).astype(f32)
    wide = jnp.where(column == size, high, wide)
    return jnp.where(column == size + 1, total - high, wide).astype(bf16)


def inverse_rms(values):
    return lax.rsqrt(jnp.mean(values * values, -1, keepdims=True) + epsilon)


def project(
    place_ref, halo_ref, tokens_ref, full_ref, vec_ref, ups_ref, fk_ref,
    normed_ref, lora_ref, query_ref, kv_ref, feat_ref, total_ref, *, size
):
    length = tokens_ref.shape[0]
    all_cols = ups_ref.shape[1]
    q_cols = query_ref.shape[1]
    gain = vec_ref[0:1]
    ups = ups_ref[...].astype(bf16)
    step = 192
    for at in range(0, length + WIN, step):
        if at == 0:
            rows = jnp.concatenate([halo_ref[...], tokens_ref[: step - WIN]], 0).astype(f32)
        else:
            rows = tokens_ref[at - WIN : at - WIN + step].astype(f32)
        normed = (rows * inverse_rms(rows) * gain).astype(bf16)
        wide = dot(normed, full_ref[...])
        lora = wide[:, all_cols:].astype(bf16)
        qkv = (wide[:, :all_cols] + dot(lora, ups)).astype(bf16)
        kv_ref[at : at + step] = qkv[:, q_cols:]
        skip = WIN if at == 0 else 0
        to = slice(at - WIN + skip, at - WIN + step)
        normed_ref[to] = normed[skip:]
        lora_ref[to] = lora[skip:]
        query_ref[to] = qkv[skip:, :q_cols]
    heads = fk_ref.shape[0]
    hidden = jnp.where(place_ref[0] == 0, WIN, 0)
    valid = lax.broadcasted_iota(jnp.int32, (length, 2 * size), 0) >= hidden
    for k in range(heads):
        keys = kv_ref[:length, k * size : (k + 1) * size]
        values = kv_ref[:length, (heads + k) * size : (heads + k + 1) * size]
        feat = softmax_pair(dot(keys, fk_ref[k].astype(bf16)))
        feat = jnp.where(valid, feat.astype(f32), 0.0).astype(bf16)
        feat_ref[:, k * 2 * size : (k + 1) * 2 * size] = feat
        total_ref[k] = dot_tn(feat, with_ones(values, 1))


def window_mask(step):
    row = lax.broadcasted_iota(jnp.int32, (step, step + WIN), 0)
    col = lax.broadcasted_iota(jnp.int32, (step, step + WIN), 1)
    return (col > row) & (col <= row + WIN), col


def early_mask(rows, cols):
    row = lax.broadcasted_iota(jnp.int32, (rows, cols), 0)
    col = lax.broadcasted_iota(jnp.int32, (rows, cols), 1)
    return col <= row + (cols - rows)


def local_attention(place_ref, q_ref, kv_ref, fq_ref, kfeat_ref, *outs, size):
    kv_heads = kfeat_ref.shape[1] // (2 * size)
    group = fq_ref.shape[0] // kv_heads
    length = kfeat_ref.shape[0]
    step = STEP
    hidden = jnp.where(place_ref[0] == 0, WIN, 0)
    in_window, col = window_mask(step)
    for k in range(kv_heads):
        acc_ref, feat_ref = outs[k], outs[kv_heads + k]
        keys = kv_ref[:, k * size : (k + 1) * size]
        values = with_ones(kv_ref[:, (kv_heads + k) * size : (kv_heads + k + 1) * size], 1)
        kfeat = kfeat_ref[:, k * 2 * size : (k + 1) * 2 * size]
        for g in range(group):
            h = k * group + g
            query = q_ref[:, h * size : (h + 1) * size]
            feat = softmax_pair(dot(query, fq_ref[h].astype(bf16)))
            feat_ref[:, g * 2 * size : (g + 1) * 2 * size] = feat
            query = (query.astype(f32) * size ** (-0.5)).astype(bf16)
            for at in range(0, length, step):
                end = at + step
                mask = in_window & (col >= hidden) if at == 0 else in_window
                weight = jnp.where(mask, jnp.exp(dot_nt(query[at:end], keys[at : end + WIN])), 0.0)
                linear = dot_nt(feat[at:end], kfeat[:end])
                linear = jnp.where(early_mask(step, end), linear, 0.0)
                acc = dot(weight.astype(bf16), values[at : end + WIN])
                acc = acc + dot(linear.astype(bf16), values[:end])
                acc_ref[at:end, g * 2 * size : (g + 1) * 2 * size] = acc


def finish_attention(
    lane_ref, *refs, size, kv_heads
):
    accs, feats = refs[:kv_heads], refs[kv_heads : 2 * kv_heads]
    state_ref, out_w_ref, down_ref = refs[2 * kv_heads : 2 * kv_heads + 3]
    total_ref, out_ref, keep_ref, send_ref = refs[2 * kv_heads + 3 :]
    group = accs[0].shape[1] // (2 * size)
    for k in range(kv_heads):
        state = split_column(state_ref[k], size)
        for g in range(group):
            cols = slice(g * 2 * size, (g + 1) * 2 * size)
            h = k * group + g
            acc = accs[k][:, cols] + dot(feats[k][:, cols], state)
            total_ref[:, h * 2 * size : (h + 1) * 2 * size] = acc
            under = acc[:, size : size + 1] + acc[:, size + 1 : size + 2]
            out_ref[:, h * size : (h + 1) * size] = (acc[:, :size] / under).astype(bf16)
    chunk = keep_ref.shape[0] // 2
    for ref, masks in ((send_ref, (1, 3)), (keep_ref, (0, 2))):
        rows = [out_ref[pl.ds(pl.multiple_of(jnp.bitwise_xor(lane_ref[0], m) * chunk, chunk), chunk)] for m in masks]
        rows = jnp.concatenate(rows, 0)
        width = out_w_ref.shape[1]
        ref[:, :width] = dot(rows, out_w_ref[...]).astype(bf16)
        ref[:, width:] = dot(rows, down_ref[...].astype(bf16)).astype(bf16)


def residual_norm(near_ref, got_ref, tokens_ref, vec_ref, middle_ref, normed_ref, lora_ref):
    width = tokens_ref.shape[1]
    branch = near_ref[...].astype(f32) + got_ref[...].astype(f32)
    rank = vec_ref.shape[0] - 8
    lora = branch[:, width:].astype(bf16)
    lora_ref[...] = lora
    ups = vec_ref[2 : 2 + rank].astype(bf16)
    middle = tokens_ref[...].astype(f32) + branch[:, :width] + dot(lora[:, :rank], ups)
    middle_ref[...] = middle
    normed_ref[...] = (middle * inverse_rms(middle) * vec_ref[1:2]).astype(bf16)


def residual_norm_back(
    near_ref, one_ref, two_ref, three_ref, middle_ref, vec_ref, dy_ref, lora_ref,
    grad_ref, branch_ref, gain_ref, up_ref
):
    grad = near_ref[...].astype(f32) + one_ref[...].astype(f32)
    grad = grad + (two_ref[...].astype(f32) + three_ref[...].astype(f32))
    middle = middle_ref[...]
    scale = inverse_rms(middle)
    rank = vec_ref.shape[0] - 8
    gain_ref[...] = jnp.broadcast_to(jnp.sum(grad * middle * scale, 0, keepdims=True), gain_ref.shape)
    scaled = grad * vec_ref[1:2]
    mean = jnp.mean(scaled * middle, -1, keepdims=True)
    total = dy_ref[...].astype(f32) + scale * scaled - middle * (scale * scale * scale * mean)
    grad_ref[...] = total
    low = total.astype(bf16)
    branch_ref[...] = low
    up_ref[...] = dot_tn(lora_ref[...], low)[:rank]


def attended_back(
    lane_ref, own_ref, side_ref, cross_ref, far_ref, out_w_ref, down_ref, vec_ref, total_ref, *refs, size, kv_heads
):
    feats = refs[:kv_heads]
    tops = refs[kv_heads : 2 * kv_heads]
    state_ref, rows_ref, grad_ref = refs[2 * kv_heads :]
    width = own_ref.shape[1]
    rank = vec_ref.shape[0] - 8
    chunk = own_ref.shape[0]
    ups = vec_ref[2 : 2 + rank].astype(bf16)
    for pieces, masks in (((own_ref, side_ref), (0, 2)), ((cross_ref, far_ref), (1, 3))):
        rows = jnp.concatenate([r[...] for r in pieces], 0)
        lora = dot_nt(rows, ups).astype(bf16)
        lora = jnp.concatenate([lora.astype(f32), jnp.zeros((2 * chunk, LANES - rank), f32)], 1).astype(bf16)
        wide = jnp.concatenate([rows, lora], 1)
        grad = dot_nt(rows, out_w_ref[...]) + dot_nt(lora, down_ref[...].astype(bf16))
        for i, m in enumerate(masks):
            to = pl.ds(pl.multiple_of(jnp.bitwise_xor(lane_ref[0], m) * chunk, chunk), chunk)
            rows_ref[to] = wide[i * chunk : (i + 1) * chunk]
            grad_ref[to] = grad[i * chunk : (i + 1) * chunk]
    group = feats[0].shape[1] // (2 * size)
    for k in range(kv_heads):
        state = None
        for g in range(group):
            h = k * group + g
            cols = slice(g * 2 * size, (g + 1) * 2 * size)
            total = total_ref[:, h * 2 * size : (h + 1) * 2 * size]
            under = total[:, size : size + 1] + total[:, size + 1 : size + 2]
            grad = grad_ref[:, h * size : (h + 1) * size] / under
            grad_under = -jnp.sum(grad * total[:, :size], -1, keepdims=True) / under
            wide = jnp.concatenate([grad, jnp.broadcast_to(grad_under, grad.shape)], 1)
            column = lax.broadcasted_iota(jnp.int32, wide.shape, 1)
            wide = split_column(jnp.where(column > size, 0.0, wide), size)
            tops[k][:, cols] = wide
            term = dot_tn(feats[k][:, cols], wide)
            state = term if state is None else state + term
        state_ref[k] = state


def local_back(
    place_ref, q_ref, kv_ref, fq_ref, kfeat_ref, feat_ref, top_ref, state_ref,
    gq_ref, gk_ref, gv_ref, gkfeat_ref, gfq_ref, *, size, k
):
    kv_heads = kfeat_ref.shape[1] // (2 * size)
    group = fq_ref.shape[0] // kv_heads
    length = kfeat_ref.shape[0]
    step = STEP
    hidden = jnp.where(place_ref[0] == 0, WIN, 0)
    in_window, col = window_mask(step)
    gk_ref[...] = jnp.zeros_like(gk_ref)
    gv_ref[...] = jnp.zeros_like(gv_ref)
    gkfeat_ref[...] = jnp.zeros_like(gkfeat_ref)
    keys = kv_ref[:, k * size : (k + 1) * size]
    values = with_ones(kv_ref[:, (kv_heads + k) * size : (kv_heads + k + 1) * size], 2)
    kfeat = kfeat_ref[:, k * 2 * size : (k + 1) * 2 * size]
    state = state_ref[k]
    column = lax.broadcasted_iota(jnp.int32, state.shape, 1)
    norm = state[:, size : size + 1]
    state = jnp.where((column == size) | (column == size + 1), norm, state).astype(bf16)
    for g in range(group):
        h = k * group + g
        matrix = fq_ref[h].astype(bf16)
        query = q_ref[:, h * size : (h + 1) * size]
        scaled = (query.astype(f32) * size ** (-0.5)).astype(bf16)
        cols = slice(g * 2 * size, (g + 1) * 2 * size)
        gfq = None
        for at in range(0, length, step):
            end = at + step
            feat = feat_ref[at:end, cols]
            top = top_ref[at:end, cols]
            mask = in_window & (col >= hidden) if at == 0 else in_window
            near = keys[at : end + WIN]
            weight = jnp.where(mask, jnp.exp(dot_nt(scaled[at:end], near)), 0.0)
            grad = (dot_nt(top, values[at : end + WIN]) * weight).astype(bf16)
            gq = dot(grad, near) * size ** (-0.5)
            gk_ref[at : end + WIN] += dot_tn(grad, scaled[at:end])
            gv_ref[at : end + WIN] += dot_tn(weight.astype(bf16), top)
            early = early_mask(step, end)
            linear = jnp.where(early, dot_nt(feat, kfeat[:end]), 0.0).astype(bf16)
            grad = jnp.where(early, dot_nt(top, values[:end]), 0.0).astype(bf16)
            gfeat = dot(grad, kfeat[:end]) + dot_nt(top, state)
            gkfeat_ref[:end] += dot_tn(grad, feat)
            gv_ref[:end] += dot_tn(linear, top)
            mix = softmax_pair_back(feat, gfeat)
            gq_ref[at:end, g * size : (g + 1) * size] = (gq + dot_nt(mix, matrix)).astype(bf16)
            term = dot_tn(query[at:end], mix)
            gfq = term if gfq is None else gfq + term
        gfq_ref[g] = gfq


def key_back(kv_ref, fk_ref, kfeat_ref, later_ref, *refs, size):
    heads = fk_ref.shape[0]
    gks, gvs, gkfeats = refs[:heads], refs[heads : 2 * heads], refs[2 * heads : 3 * heads]
    gkv_ref, halo_ref, gfk_ref = refs[3 * heads :]
    length = kfeat_ref.shape[0]
    for k in range(heads):
        keys = kv_ref[:length, k * size : (k + 1) * size]
        values = with_ones(kv_ref[:length, (heads + k) * size : (heads + k + 1) * size], 2)
        cols = slice(k * 2 * size, (k + 1) * 2 * size)
        later = later_ref[k]
        column = lax.broadcasted_iota(jnp.int32, later.shape, 1)
        norm = later[:, size : size + 1] + later[:, size + 1 : size + 2]
        later = split_column(jnp.where(column == size, norm, later), size)
        kfeat = kfeat_ref[:, cols]
        mix = softmax_pair_back(kfeat, gkfeats[k][...] + dot_nt(values, later))
        gk, gv = slice(k * size, (k + 1) * size), slice((heads + k) * size, (heads + k + 1) * size)
        gkv_ref[:, gk] = gks[k][...]
        gkv_ref[:length, gk] += dot_nt(mix, fk_ref[k].astype(bf16))
        gkv_ref[:, gv] = gvs[k][:, :size]
        gkv_ref[:length, gv] += dot(kfeat, later)[:, :size]
        gfk_ref[k] = dot_tn(keys, mix)
    halo_ref[...] = gkv_ref[:WIN].astype(bf16)


def project_back(
    lane_ref, *refs, kv_heads
):
    gqs = refs[:kv_heads]
    gkv_ref, back_ref, ups_ref, full_ref, tokens_ref, normed_ref, lora_ref = refs[kv_heads : kv_heads + 7]
    gqkv_ref, keep_ref, send_ref, gain_ref, down_ref, up_ref, ext_ref = refs[kv_heads + 7 :]
    length = tokens_ref.shape[0]
    each = gqs[0].shape[1]
    q_cols = each * kv_heads
    all_cols = ups_ref.shape[1]
    for k in range(kv_heads):
        ext_ref[:, k * each : (k + 1) * each] = gqs[k][...]
    ext_ref[: length - WIN, q_cols:all_cols] = gkv_ref[WIN:length].astype(bf16)
    ext_ref[length - WIN :, q_cols:all_cols] = (gkv_ref[length:] + back_ref[...].astype(f32)).astype(bf16)
    gqkv_ref[...] = ext_ref[:, :all_cols]
    ext_ref[:, all_cols:] = dot_nt(ext_ref[:, :all_cols], ups_ref[...].astype(bf16)).astype(bf16)
    down_ref[...] = dot_tn(ext_ref[:, all_cols:], normed_ref[...])[: down_ref.shape[0]]
    up_ref[...] = dot_tn(lora_ref[...], ext_ref[:, :all_cols])[: up_ref.shape[0]]
    chunk = keep_ref.shape[0] // 2
    width = keep_ref.shape[1]
    gain_ref[...] = jnp.zeros_like(gain_ref)
    for ref, masks in ((send_ref, (1, 3)), (keep_ref, (0, 2))):
        for i, m in enumerate(masks):
            at = pl.ds(pl.multiple_of(jnp.bitwise_xor(lane_ref[0], m) * chunk, chunk), chunk)
            rows = tokens_ref[at].astype(f32)
            scale = inverse_rms(rows)
            grad = dot_nt(ext_ref[at], full_ref[...])
            ref[i * chunk : (i + 1) * chunk] = grad.astype(bf16)
            gain_ref[...] += jnp.broadcast_to(
                jnp.sum(grad * rows * scale, 0, keepdims=True), gain_ref.shape
            )


def norm_back(near_ref, got_ref, tokens_ref, vec_ref, middle_ref, out_ref):
    grad = near_ref[...].astype(f32) + got_ref[...].astype(f32)
    values = tokens_ref[...].astype(f32)
    scale = inverse_rms(values)
    scaled = grad * vec_ref[0:1]
    mean = jnp.mean(scaled * values, -1, keepdims=True)
    total = middle_ref[...] + scale * scaled - values * (scale * scale * scale * mean)
    out_ref[...] = total.astype(bf16)


def units_kernel(*refs):
    gu_ref, down_ref, keep_ref, send_ref, hkeep_ref, hsend_ref, ggu_ref = refs[8:]
    half = keep_ref.shape[0]
    units = down_ref.shape[0]
    width = down_ref.shape[1]
    step = 256
    normed = jnp.concatenate([r[...] for r in refs[:4]], 0)
    grad_out = jnp.concatenate([r[...] for r in refs[4:8]], 0)
    for at in range(0, units, step):
        one = slice(at, at + step)
        two = slice(units + at, units + at + step)
        gate = dot(normed, gu_ref[:, one])
        up = dot(normed, gu_ref[:, two])
        grad = dot_nt(grad_out, down_ref[one])
        sigma = 1.0 / (1.0 + jnp.exp(-gate))
        active = gate * sigma
        hidden = (active * up).astype(bf16)
        hkeep_ref[:, one] = hidden[:half]
        hsend_ref[:, one] = hidden[half:]
        ggu_ref[:, one] = (grad * up * sigma * (1.0 + gate * (1.0 - sigma))).astype(bf16)
        ggu_ref[:, two] = (grad * active).astype(bf16)
    for at in range(0, width, 512):
        cols = slice(at, at + 512)
        grad = dot_nt(ggu_ref[...], gu_ref[cols]).astype(bf16)
        keep_ref[:, cols] = grad[:half]
        send_ref[:, cols] = grad[half:]


def blocks_of_product(place_ref, *refs, lefts, rights, groups, picks):
    left, right = refs[:lefts], refs[lefts : lefts + rights]
    out = refs[-1]
    rows = out.shape[0] // len(picks)

    def joined(pieces):
        return jnp.concatenate(pieces, 0) if len(pieces) > 1 else pieces[0]

    for i, pick in enumerate(picks):
        at = pl.multiple_of(jnp.bitwise_xor(place_ref[0], pick) * rows, rows)
        total = None
        for d in range(groups):
            own = slice(d * lefts // groups, (d + 1) * lefts // groups)
            part = joined([r[:, pl.ds(at, rows)] for r in left[own]])
            own = slice(d * rights // groups, (d + 1) * rights // groups)
            term = dot_tn(part, joined([r[...] for r in right[own]]))
            total = term if total is None else total + term
        out[i * rows : (i + 1) * rows] = total.astype(bf16)


def out_blocks(place_ref, left_ref, right_ref, keep_ref, send_ref, sum_ref, *, pair):
    sum_ref[...] = dot_tn(left_ref[...], right_ref[...])
    count = RING * pair
    rows = sum_ref.shape[0] // count
    for i in range(count):
        at = pl.multiple_of(jnp.bitwise_xor(place_ref[0], i) * rows, rows)
        d, beta = i // pair, i % pair
        part = sum_ref[pl.ds(at, rows)].astype(bf16)
        d = (0, 2, 1, 3)[d]
        if beta == 0:
            keep_ref[d * rows : (d + 1) * rows] = part
        else:
            to = (beta - 1) * RING + d
            send_ref[to * rows : (to + 1) * rows] = part


def pack_small(place_ref, gfk_ref, up_ref, down_ref, outu_ref, two_ref, one_ref, *refs, kv_heads, group):
    gfqs, out_ref = refs[:kv_heads], refs[-1]
    count = out_ref.shape[0]
    size = gfk_ref.shape[2]
    each = size // count
    rank = up_ref.shape[0] // 3
    q_cols = kv_heads * group * size
    kv_cols = kv_heads * size
    q_each, kv_each = q_cols // count, kv_cols // count
    vec_cols = down_ref.shape[1] // count
    vec_rows = 48

    def wide(value, rows):
        if value.shape[1] < LANES:
            value = jnp.concatenate([value, jnp.zeros((value.shape[0], LANES - value.shape[1]), f32)], 1)
        if value.shape[0] < rows:
            value = jnp.concatenate([value, jnp.zeros((rows - value.shape[0], LANES), f32)], 0)
        return value

    for s in range(count):
        own = slice(s * each, (s + 1) * each)
        fq = jnp.concatenate([gfqs[k][g, own] for k in range(kv_heads) for g in range(group)], 0)
        fk = jnp.concatenate([gfk_ref[k, own] for k in range(kv_heads)], 0)
        kv = [
            up_ref[(c + 1) * rank : (c + 2) * rank, q_cols + c * kv_cols + s * kv_each : q_cols + c * kv_cols + (s + 1) * kv_each]
            for c in range(2)
        ]
        q = up_ref[:rank, s * q_each : (s + 1) * q_each]
        groups = [wide(fq, fq.shape[0]), wide(fk, 16), wide(jnp.concatenate(kv, 0), 16), wide(q, 16)]
        for at in range(s * vec_cols, (s + 1) * vec_cols, min(LANES, vec_cols)):
            cols = slice(at, at + min(LANES, vec_cols))
            vec = [down_ref[:, cols], outu_ref[:, cols], two_ref[:1, cols], one_ref[:1, cols]]
            groups.append(wide(jnp.concatenate(vec, 0), vec_rows))
        away = jnp.bitwise_xor(place_ref[0], s)
        to, bit = 0, 1
        while bit < count:
            to = to + jnp.where((away & bit) != 0, count // (2 * bit), 0)
            bit *= 2
        out_ref[pl.ds(to, 1)] = jnp.concatenate(groups, 0).astype(bf16)[None]


def per_device(
    tokens,
    attention_norm_gain,
    query_weight,
    key_value_weight,
    output_weight,
    adapter_down_matrices,
    adapter_query_up,
    adapter_key_value_up,
    adapter_output_down,
    adapter_output_up,
    query_feature_matrix,
    key_feature_matrix,
    feedforward_norm_gain,
    gate_weight,
    up_weight,
    down_weight,
    cotangent,
):
    count = lax.axis_size(SEQ)
    pair = count // RING
    place = lax.axis_index(SEQ)
    along, beside = place // pair, place % pair
    lane = lax.axis_index("kv")
    unused, length, width = tokens.shape
    depth, q_cols = query_weight.shape
    kv_cols = key_value_weight.shape[2]
    heads, head_size = query_feature_matrix.shape[0], query_feature_matrix.shape[2]
    kv_heads = key_feature_matrix.shape[0]
    group = heads // kv_heads
    rank = adapter_query_up.shape[0]
    all_cols = q_cols + 2 * kv_cols
    wide_size = 2 * head_size
    chunk = length // lax.axis_size("kv")
    rows_out = output_weight.shape[0]
    units_each = down_weight.shape[0]
    units = gate_weight.shape[1] // RING
    here = place.astype(jnp.int32)[None]
    lane_here = lane.astype(jnp.int32)[None]
    order = [place ^ i for i in range(count)]
    nears = [lane ^ k for k in (0, 2, 1, 3)]
    rings = [d * pair for d in range(RING)]
    x = tokens[0]
    dy = cotangent[0]

    def across(array, *gates):
        result = [array]
        bit = 1
        while bit < pair:
            result = result + [trade(after(a, *gates), SEQ, bit) for a in result]
            bit *= 2
        return result

    def across_sum(parts, *gates):
        bit = pair // 2
        while bit:
            parts = [
                add_low(parts[i], after(trade(parts[i + bit], SEQ, bit), *gates)) for i in range(bit)
            ]
            bit //= 2
        return parts[0]

    parameters = [
        jnp.swapaxes(adapter_down_matrices, 1, 2),
        query_feature_matrix.reshape(-1, head_size),
        adapter_output_down.T,
        key_feature_matrix.reshape(-1, head_size),
        adapter_key_value_up.reshape(2 * rank, -1),
        adapter_query_up,
        jnp.stack([attention_norm_gain, feedforward_norm_gain]),
        adapter_output_up,
    ]
    packed = pl.pallas_call(
        pack_weights,
        out_shape=shape((depth, all_cols + LANES), bf16),
        in_specs=[pl.BlockSpec(memory_space=pltpu.HBM)] * (2 + len(parameters)),
        out_specs=pl.BlockSpec(memory_space=pltpu.VMEM),
        scratch_shapes=[pltpu.VMEM(p.shape, bf16) for p in parameters]
        + [pltpu.SemaphoreType.DMA((3 + len(parameters),))],
        compiler_params=pltpu.CompilerParams(vmem_limit_bytes=12 * 2**20),
    )(query_weight, key_value_weight, *parameters)
    got = [packed, trade(packed, SEQ, rings[1]), trade(packed, SEQ, rings[2])]
    halo = moved(x[length - WIN :], SEQ, 1)
    pieces = [across(packed)]

    cuts = own_call(
        cut_units,
        [shape((depth, 2 * units), bf16)] * RING,
        [jnp.stack([along ^ d for d in range(RING)]).astype(jnp.int32), gate_weight, up_weight],
        1,
    )
    own_gu = across(cuts[0], got[2], pieces[0][-1], halo)
    pieces.append(across(got[1]))
    pieces.append(across(got[2]))
    got.append(trade(got[2], SEQ, rings[1]))
    pieces.append(across(got[3]))
    last_piece = pieces[3][-1]
    out_got = [output_weight] + [trade(after(output_weight, pieces[1][-1], pieces[0][-1], halo), SEQ, m) for m in rings[1:3]]
    gu_got = [cuts[0], None, None, None]
    gu_got[2] = trade(after(cuts[2], *out_got[1:]), SEQ, rings[2])
    out_got.append(trade(out_got[2], SEQ, rings[1]))
    gu_got[1] = trade(after(cuts[1], out_got[3]), SEQ, rings[1])
    out_first = across(jnp.concatenate(out_got[:2], 0), last_piece)

    own_x = block(x, lane, chunk)
    own_dy = block(dy, lane, chunk)
    dy_blocks = [[block(dy, k, chunk) for k in nears]]
    full, fq_w, fk_w, ups, out_down, vecs = placed(
        [pieces[d][b] for d in range(RING) for b in range(pair)],
        depth,
        order,
        functools.partial(unpack_weights, count=count),
        [
            shape((heads, head_size, head_size), f32),
            shape((kv_heads, head_size, head_size), f32),
            shape((LANES, all_cols), f32),
            shape((q_cols, LANES), f32),
            shape((8 + rank, width), f32),
        ],
        deps=[own_x, own_gu[-1]] + dy_blocks[0],
    )

    normed, lora, query, kv_ext, key_feat, totals = own_call(
        functools.partial(project, size=head_size),
        [
            shape((length, width), bf16),
            shape((length, LANES), bf16),
            shape((length, q_cols), bf16),
            shape((length + WIN, 2 * kv_cols), bf16),
            shape((length, kv_heads * wide_size), bf16),
            shape((kv_heads, wide_size, wide_size), f32),
        ],
        [here, halo, x, full, vecs, ups, fk_w],
        1,
    )
    def running(total, sign, between, beside=True):
        result = jnp.zeros_like(total)
        results, steps = [], []
        bit = 1
        while bit < count:
            other = trade(total, SEQ, bit)
            if len(results) < len(between):
                results.append(between[len(results)](*(steps[-1:] if beside else [other])))
                if beside:
                    other = after(other, results[-1][0])
            steps.append(other)
            mine = (place & bit) != 0 if sign > 0 else (place & bit) == 0
            result = result + jnp.where(mine, other, 0.0)
            total = total + other
            bit *= 2
        return result, results, steps

    states, unused, steps = running(totals, 1, [])
    local = own_call(
        functools.partial(local_attention, size=head_size),
        [shape((length, group * wide_size), f32)] * kv_heads
        + [shape((length, group * wide_size), bf16)] * kv_heads,
        [here, query, kv_ext, fq_w, key_feat],
        1,
        deps=[steps[1], gu_got[1], gu_got[2]],
    )
    accs, feats = list(local[:kv_heads]), list(local[kv_heads:])
    out_second = across(jnp.concatenate(out_got[2:], 0), steps[0])
    gu_got[3] = trade(after(cuts[3], states), SEQ, rings[3])
    dy_got = [None, trade(after(own_dy, states), SEQ, rings[1])]
    out_w = placed(
        out_first + out_second,
        rows_out,
        [order[rings[d] + b] for b in range(pair) for d in (0, 1)]
        + [order[rings[d] + b] for b in range(pair) for d in (2, 3)],
    )
    gu_mid = across(jnp.concatenate([gu_got[1], gu_got[2]], 0))
    tops, attended, keep, send = own_call(
        functools.partial(finish_attention, size=head_size, kv_heads=kv_heads),
        [
            shape((length, heads * wide_size), f32),
            shape((length, q_cols), bf16),
            shape((2 * chunk, width + LANES), bf16),
            shape((2 * chunk, width + LANES), bf16),
        ],
        [lane_here] + accs + feats + [states, out_w, out_down],
        1,
        deps=[],
    )
    downs = across(down_weight, gu_mid[-1])

    def kv_sums(keep, send, *gates):
        other = after(trade(send, "kv", 1), *gates)
        near = add_low(keep[:chunk], other[:chunk])
        side = add_low(keep[chunk:], other[chunk:])
        return near, trade(side, "kv", 2)

    def kv_all(own, *gates):
        side = trade(own, "kv", 2)
        return own, side, trade(own, "kv", 1), trade(after(side, *gates), "kv", 1)

    near, other = kv_sums(keep, send)
    middle, normed_two, lora_out = own_call(
        residual_norm,
        [shape((chunk, width), f32), shape((chunk, width), bf16), shape((chunk, LANES), bf16)],
        [near, other, own_x, vecs],
        deps=[gu_mid[-1]],
    )

    n_got = [normed_two, None, None, None]
    n_got[2] = trade(normed_two, SEQ, rings[2])
    n_got[1] = trade(normed_two, SEQ, rings[1])
    gu_last = across(gu_got[3])
    n_first = kv_all(normed_two, gu_mid[-1], downs[-1], gu_last[-1])
    n_got[3] = trade(n_got[2], SEQ, rings[1])
    dy_got.append(trade(after(own_dy, n_got[1]), SEQ, rings[2]))
    dy_got.append(trade(after(dy_got[2], n_got[3]), SEQ, rings[1]))
    dy_blocks.append(kv_all(after(dy_got[1], normed_two)))
    gu_w = placed(
        [after(g, normed_two) for g in own_gu + gu_mid + gu_last],
        depth,
        [order[b] for b in range(pair)]
        + [order[rings[d] + b] for b in range(pair) for d in (1, 2)]
        + [order[rings[3] + b] for b in range(pair)],
    )
    down_w = placed([after(w, normed_two) for w in downs], units_each, [beside ^ b for b in range(pair)])
    n_blocks = []
    keeps, hiddens, ggus = [], [], []
    sums = [None] * RING
    halves = [None] * RING
    for d in range(RING):
        n_blocks.append(n_first if d == 0 else kv_all(n_got[d]))
        if d == 0:
            ready = []
        elif d == 1:
            ready = [n_got[3], dy_got[2], kv_all(n_got[2])[1]]
        else:
            ready = [halves[d - 2][0], halves[d - 2][1]]
        if d == 2:
            ready.append(kv_all(n_got[3])[1])
        if d > 1:
            dy_blocks.append(kv_all(dy_got[d]))
        keep, send, hkeep, hsend, ggu = own_call(
            units_kernel,
            [shape((2 * chunk, width), bf16)] * 2
            + [shape((2 * chunk, units), bf16)] * 2
            + [shape((4 * chunk, 2 * units), bf16)],
            list(n_blocks[d]) + list(dy_blocks[d]) + [gu_w, down_w],
            deps=ready + keeps[-1:],
        )
        keeps.append(keep)
        other = trade(send, "kv", 1)
        halves[d] = (add_low(keep[:chunk], other[:chunk]), add_low(keep[chunk:], other[chunk:]))
        hiddens.append((hkeep, hsend))
        ggus.append(ggu)
    def product(left, right, picks, rows, groups=RING, at=here, deps=()):
        if rows % LANES == 0:
            return own_call(
                functools.partial(
                    blocks_of_product, lefts=len(left), rights=len(right), groups=groups, picks=picks
                ),
                [shape((rows * len(picks), right[0].shape[1]), bf16)],
                [at] + left + right,
                1,
                deps=deps,
            )[0]
        result = dot_tn(jnp.concatenate(left, 0), jnp.concatenate(right, 0)).astype(bf16)
        return jnp.concatenate([block(result, at[0] ^ i, rows) for i in picks], 0)

    n_all = [p for n in n_blocks for p in n]
    picks = [[m + b for m in rings] for b in range(pair)]
    gu_parts = [None] * pair
    for b in range(1, pair):
        gu_parts[b] = [product(n_all, ggus, p, depth, deps=halves[3]) for p in (picks[b][2:], picks[b][:2])]
    firsts = [p for part in gu_parts[1:] for p in part]
    sums = [None] * RING
    for d in (0, 3, 2, 1):
        side = halves[d][1]
        sums[d] = add_low(after(halves[d][0], *firsts) if d == 3 else halves[d][0], trade(side, "kv", 2))
    rest = [trade(sums[d], SEQ, rings[d]) for d in (1, 2, 3)]
    gu_parts[0] = [product(n_all, ggus, p, depth, deps=[sums[3]]) for p in (picks[0][2:], picks[0][:2])]
    far_cols = across_sum([p[0] for p in gu_parts])
    hidden_all = [p for h in hiddens for p in h]
    dy_all = [p for b in dy_blocks for p in b]
    beside_here = beside.astype(jnp.int32)[None]
    down_parts = [None] * pair
    for b in reversed(range(pair)):
        down_parts[b] = product(
            hidden_all, dy_all, [b], units_each, RING, beside_here, [sums[3]]
        )
    grad_middle, grad_branch, gain_two, out_up_part = own_call(
        residual_norm_back,
        [
            shape((chunk, width), f32),
            shape((chunk, width), bf16),
            shape((8, width), f32),
            shape((rank, width), f32),
        ],
        [sums[0]] + rest + [middle, vecs, own_dy, lora_out],
        deps=gu_parts[0] + down_parts + [far_cols],
    )

    all_branch = kv_all(grad_branch)

    hkeep = jnp.concatenate([h[0] for h in hiddens], 0)
    hsend = jnp.concatenate([h[1] for h in hiddens], 0)
    down_send = dot(after(hsend, grad_branch), down_w).astype(bf16)
    down_keep = dot(after(hkeep, grad_branch), down_w).astype(bf16)
    near_cols = across_sum([p[1] for p in gu_parts])
    down_other = trade(down_send, "kv", 1)
    gate_parts = [near_cols[:depth], None, None, None]
    gate_parts[2] = trade(far_cols[:depth], SEQ, rings[2])
    gate_parts[3] = trade(far_cols[depth:], SEQ, rings[3])
    results = own_call(
        functools.partial(attended_back, size=head_size, kv_heads=kv_heads),
        [shape((length, group * wide_size), bf16)] * kv_heads
        + [shape((kv_heads, wide_size, wide_size), f32), shape((length, width + LANES), bf16)],
        [lane_here] + list(all_branch) + [out_w, out_down, vecs, tops] + feats,
        1,
        [pltpu.VMEM((length, q_cols), f32)],
        deps=[],
    )
    grad_tops, grad_state, branch_rows = results[:kv_heads], results[kv_heads], results[kv_heads + 1]
    other = down_other.reshape(RING, 2, chunk, width)
    down_keep = down_keep.reshape(RING, 2, chunk, width)
    near = add_low(down_keep[:, 0], other[:, 0])
    side = add_low(down_keep[:, 1], other[:, 1])
    high = trade(after(side[2:], all_branch[1]), "kv", 2)
    down_sum = across_sum(down_parts)
    out_keep, out_send = own_call(
        functools.partial(out_blocks, pair=pair),
        [
            shape((RING * rows_out, width + LANES), bf16),
            shape(((pair - 1) * RING * rows_out, width + LANES), bf16),
        ],
        [here, attended, branch_rows],
        1,
        [pltpu.VMEM((q_cols, width + LANES), f32)],
    )
    out_parts = [out_keep] + [
        out_send[b * RING * rows_out : (b + 1) * RING * rows_out] for b in range(pair - 1)
    ]

    def attend_back(k, *step):
        return own_call(
            functools.partial(local_back, size=head_size, k=k),
            [
                shape((length, group * head_size), bf16),
                shape((length + WIN, head_size), f32),
                shape((length + WIN, wide_size), f32),
                shape((length, wide_size), f32),
                shape((group, head_size, head_size), f32),
            ],
            [here, query, kv_ext, fq_w, key_feat, feats[k], grad_tops[k], states],
            1,
            deps=list(step) + ([high] if k else [side, out_send, down_sum]),
        )

    later, local, steps = running(grad_state, -1, [functools.partial(attend_back, k) for k in range(kv_heads)])
    gate_parts[1] = trade(near_cols[depth:], SEQ, rings[1])
    low = trade(after(side[:2], high), "kv", 2)
    low_first = low
    high = add_low(near[2:], high)
    low = add_low(near[:2], low)
    out_sum = across_sum([out_keep] + [after(p, steps[0]) for p in out_parts[1:]], local[0][0])
    mixed = trade(jnp.concatenate([high[1], low[1]], 0), SEQ, rings[1])
    out_half = 2 * rows_out
    out_other = trade(out_sum[out_half:], SEQ, rings[1])
    grad_kv, halo_back, grad_fk = own_call(
        functools.partial(key_back, size=head_size),
        [
            shape((length + WIN, 2 * kv_cols), f32),
            shape((WIN, 2 * kv_cols), bf16),
            shape((kv_heads, head_size, head_size), f32),
        ],
        [kv_ext, fk_w, key_feat, later] + [l[1] for l in local] + [l[2] for l in local] + [l[3] for l in local],
        deps=[low_first],
    )
    returned = moved(halo_back, SEQ, -1)

    gqkv, grad_keep, grad_send, gain_one, lora_down, up_all, ext = own_call(
        functools.partial(project_back, kv_heads=kv_heads),
        [
            shape((length, all_cols), bf16),
            shape((2 * chunk, width), bf16),
            shape((2 * chunk, width), bf16),
            shape((8, width), f32),
            shape((3 * rank, width), f32),
            shape((3 * rank, all_cols), f32),
            shape((length, all_cols + LANES), bf16),
        ],
        [lane_here] + [l[0] for l in local] + [grad_kv, returned, ups, full, x, normed, lora],
        1,
    )
    near, other = kv_sums(grad_keep, grad_send)
    qkv_parts = [None] * pair
    for b in reversed(range(pair)):
        qkv_parts[b] = [product([normed], [gqkv], p, depth, 1, deps=[near]) for p in (picks[b][2:], picks[b][:2])]

    qkv_high = across_sum([p[0] for p in qkv_parts])
    qkv_low = across_sum([p[1] for p in qkv_parts])
    (own_grad,) = own_call(
        norm_back, [shape((chunk, width), bf16)], [near, other, own_x, vecs, grad_middle],
        deps=[qkv_high],
    )
    all_grad = kv_all(own_grad)

    vec_cols = width // count
    fq_rows = heads * head_size // count
    fk_rows = kv_heads * head_size // count
    small_rows = fq_rows + 48 + 48 * max(1, vec_cols // LANES)
    (small,) = own_call(
        functools.partial(pack_small, kv_heads=kv_heads, group=group),
        [shape((count, small_rows, LANES), bf16)],
        [here, grad_fk, up_all, lora_down, out_up_part, gain_two, gain_one] + [l[4] for l in local],
        1,
        deps=[own_grad],
    )
    half, bit = count // 2, 1
    while half:
        small = add_low(small[:half], trade(small[half:], SEQ, bit))
        half, bit = half // 2, 2 * bit
    qkv_far = add_low(qkv_high[:depth], trade(qkv_high[depth:], SEQ, rings[1]))
    qkv_near = add_low(qkv_low[:depth], trade(qkv_low[depth:], SEQ, rings[1]))
    grad_w = qkv_near.astype(f32) + trade(qkv_far, SEQ, rings[2]).astype(f32)
    grad_w_query = grad_w[:, :q_cols]
    grad_w_kv = jnp.stack([grad_w[:, q_cols : q_cols + kv_cols], grad_w[:, q_cols + kv_cols :]])

    (grad_tokens,) = own_call(
        rows_placed, [shape((length, width), f32)], [jnp.stack(nears).astype(jnp.int32), *all_grad], 1
    )

    mixed = after(mixed, own_grad)
    high = add_low(high[0], mixed[:chunk])
    low = add_low(low[0], mixed[chunk:])
    ffn_out = add_low(low, trade(high, SEQ, rings[2])).astype(f32)
    own_out = (middle + ffn_out).astype(bf16)
    all_out = kv_all(own_out)
    (output,) = own_call(
        rows_placed, [shape((length, width), bf16)], [jnp.stack(nears).astype(jnp.int32), *all_out], 1
    )
    out_sum = add_low(after(out_sum[:out_half], own_grad), out_other)
    out_sum = add_low(out_sum[:rows_out], trade(out_sum[rows_out:], SEQ, rings[2])).astype(f32)
    grad_w_gate, grad_w_up = own_call(
        place_units,
        [shape(gate_weight.shape, f32)] * 2,
        [jnp.stack([along ^ d for d in range(RING)]).astype(jnp.int32)]
        + gate_parts,
        1,
        deps=[qkv_low],
    )

    small = small[0]
    at = fq_rows
    grad_fmap_query = small[:at, :head_size].astype(f32).reshape(query_feature_matrix.shape)
    grad_fmap_key = small[at : at + fk_rows, :head_size].astype(f32).reshape(key_feature_matrix.shape)
    at += 16
    kv_each, q_each = kv_cols // count, q_cols // count
    grad_lora_up_kv = small[at : at + 2 * rank, :kv_each].astype(f32).reshape(2, rank, kv_each)
    at += 16
    grad_lora_up_query = small[at : at + rank, :q_each].astype(f32)
    at += 16
    total = small[at:]
    for mask in (1, 2):
        total = lax.optimization_barrier(total)
        total = add_low(total, trade(total, "kv", mask))
    total = lax.optimization_barrier(total).astype(f32)
    each = min(LANES, vec_cols)
    total = jnp.concatenate(
        [total[i * 48 : (i + 1) * 48, :each] for i in range(vec_cols // each)], 1
    )
    grad_lora_down = jnp.transpose(total[: 3 * rank].reshape(3, rank, depth), (0, 2, 1))
    grad_lora_up_out = total[3 * rank : 4 * rank]
    grad_g_mlp = total[4 * rank]
    grad_g_attn = total[4 * rank + 1]
    return (
        output[None],
        grad_tokens[None],
        grad_g_attn,
        grad_w_query,
        grad_w_kv,
        out_sum[:, :width],
        grad_lora_down,
        grad_lora_up_query,
        grad_lora_up_kv,
        out_sum[:, width : width + rank],
        grad_lora_up_out,
        grad_fmap_query,
        grad_fmap_key,
        grad_g_mlp,
        grad_w_gate,
        grad_w_up,
        down_sum.astype(f32),
    )


def solution(mesh):
    devices = mesh.devices
    count, kv = devices.shape
    mesh = Mesh(devices.reshape(RING, count // RING, kv), SEQ + ("kv",))
    return jax.shard_map(
        per_device,
        mesh=mesh,
        in_specs=(
            P(None, SEQ, None),
            P(SEQ),
            P(SEQ, "kv"),
            P(None, SEQ, "kv"),
            P(("kv",) + SEQ, None),
            P(None, SEQ, None),
            P(None, ("kv",) + SEQ),
            P(None, None, ("kv",) + SEQ),
            P(("kv",) + SEQ, None),
            P(None, SEQ),
            P("kv", SEQ, None),
            P("kv", SEQ, None),
            P(SEQ),
            P(SEQ, "kv"),
            P(SEQ, "kv"),
            P(("kv",) + SEQ, None),
            P(None, SEQ, None),
        ),
        out_specs=(
            P(None, SEQ, None),
            P(None, SEQ, None),
            P(SEQ),
            P(SEQ, "kv"),
            P(None, SEQ, "kv"),
            P(("kv",) + SEQ, None),
            P(None, SEQ, None),
            P(None, ("kv",) + SEQ),
            P(None, None, ("kv",) + SEQ),
            P(("kv",) + SEQ, None),
            P(None, SEQ),
            P("kv", SEQ, None),
            P("kv", SEQ, None),
            P(SEQ),
            P(SEQ, "kv"),
            P(SEQ, "kv"),
            P(("kv",) + SEQ, None),
        ),
        check_vma=False,
    )
```
